32 devices in a mesh: dp: 4 (over y, x), expert: 8 (over z, core).
Axes of the slice: x: 2, y: 2, z: 4, core: 2. Of those that a mesh axis runs over, the one named last changes fastest.
Arguments:
- tokens: bfloat16 [2048, 2048], P('dp'), may hold values from -6 to 6
- routes: int32 [2048, 6], P('dp'), may hold values from 0 to 7, all different within a row; in each aligned block of 512 rows (0 to 511, 512 to 1023, ...) at most 512 rows name the same one
- route_weight: float32 [2048, 6], P('dp'), may hold values from 0.05 to 0.5
- w_gate: bfloat16 [32, 352, 2048], P(('dp', 'expert')), may hold values from -0.125 to 0.125
- w_up: bfloat16 [32, 352, 2048], P(('dp', 'expert')), may hold values from -0.125 to 0.125
- w_down: bfloat16 [32, 352, 2048], P(('dp', 'expert')), may hold values from -0.15625 to 0.15625
- grad_out: bfloat16 [2048, 2048], P(('dp', 'expert')), may hold values from -6 to 6
Outputs:
- mixed: bfloat16 [2048, 2048], P(('dp', 'expert'))
- grad_tokens: bfloat16 [2048, 2048], P(('dp', 'expert'))
- grad_route_weight: float32 [2048, 6], P(('dp', 'expert'))
- grad_gate: bfloat16 [32, 352, 2048], P(('dp', 'expert'))
- grad_up: bfloat16 [32, 352, 2048], P(('dp', 'expert'))
- grad_down: bfloat16 [32, 352, 2048], P(('dp', 'expert'))
The draws below stay inside these ranges and needn't reach their ends.
Inputs may be any that keep to these rules, and one draw needn't show every extreme that they name: `routes`: each row names 6 different experts. Within the 512 rows of one index of dp no expert is named by more than 512 rows.
All inputs are finite; a program needn't handle non-finite values.
Results may differ from the reference program's by a relative error of at most 0.023.
Values may be sent and summed in bfloat16 or wider, within the bound.
No kernel may reach another device: no remote copies, remote signals or barrier semaphores. Data moves between devices by JAX's collectives and lax.ppermute only.
A program may use at most 192 MiB of HBM per device.

```python
import math
import jax
import jax.numpy as jnp
import numpy as np
from jax import lax

D = 2048
FF = 1408
TOP = 6
SHARDS = 4
TOK_DP = 512
EXPERTS = 8
FF_DEV = 352
CAP = 512
TOKENS = 2048
N_DP = 4


def block_scale(stream_key, extent, split, low, largest):
    gain = 1.0
    for position, shards_of in split:
        steps = jax.random.uniform(jax.random.fold_in(jax.random.fold_in(stream_key, 6), position), (shards_of,), jnp.float32, low / len(split), largest / len(split))
        gain = gain * jnp.repeat(jnp.exp(steps), extent[position] // shards_of).reshape((-1,) + (1,) * (len(extent) - 1 - position))
    return gain


def shared_out(stream_key, own, number, rows, amount, top, bound, slope):
    sequence = jax.random.permutation(stream_key, amount)
    packed, common = load_shares(amount, rows * top, bound, slope, True), load_shares(amount, rows * top, bound, slope, False)
    places = jnp.arange(amount)

    def named(lengths, rotation):
        used = int((lengths > 0).sum())
        fixed = max(1, used // 4)
        passed = fixed + (places - fixed + rotation * (used - fixed)) % max(1, amount - fixed)
        return jnp.zeros((amount,), jnp.int32).at[sequence[jnp.where(places < fixed, places, passed)]].set(jnp.asarray(lengths, jnp.int32))

    lengths = jnp.where(number % 4 == 0, named(packed, number // 4), named(common, number - number // 4 - 1))
    mixed = jax.random.permutation(jax.random.fold_in(own, 3), amount)
    giver, taker = mixed[0:amount // 2 * 2:2], mixed[1:amount // 2 * 2:2]
    slack = jnp.minimum(lengths[giver] - 1, bound - lengths[taker]) // 2
    slack = jnp.where((giver == sequence[0]) | (taker == sequence[0]) | (lengths[taker] == 0), 0, jnp.maximum(slack, 0))
    passed = jax.random.randint(jax.random.fold_in(own, 4), (amount // 2,), 0, 1 << 20) % (slack + 1)
    lengths = lengths.at[giver].add(-passed).at[taker].add(passed)
    items = jnp.searchsorted(jnp.cumsum(lengths), jnp.arange(rows * top), side="right").astype(jnp.int32)
    listing = items.reshape(top, rows).T
    listing = listing[jax.random.permutation(jax.random.fold_in(own, 1), rows)]
    rotation = jax.random.randint(jax.random.fold_in(own, 2), (rows, 1), 0, top)
    return jnp.take_along_axis(listing, (jnp.arange(top)[None, :] + rotation) % top, axis=1)


def load_shares(count, total, reach, lean, full):
    weights = [(1 << 20) // math.isqrt(grade ** lean) + 1 for grade in range(1, count + 1)]
    largest = reach if full else min(reach, max(-(-total // count), total * weights[0] // sum(weights)))
    least = 1 if total - largest >= count - 1 else 0
    given, surplus = [largest] + [least] * (count - 1), total - largest - least * (count - 1)
    while surplus > 0:
        movable = [i for i in range(1, count) if given[i] < largest] or [i for i in range(1, count) if given[i] < reach]
        pool, left = sum([weights[i] for i in movable]), surplus
        for i in movable:
            more = min(reach - given[i], max(1, left * weights[i] // pool), surplus)
            given[i] = given[i] + more
            surplus = surplus - more
    return np.array(given)


def normal_values(stream_key, dims, scale, limit, split=(), held_as=jnp.bfloat16):
    drawn = jax.random.normal(stream_key, dims, jnp.float32) * scale
    if len(split) > 0:
        drawn = block_scale(stream_key, dims, split, -0.22, 0.18) * drawn
    return jnp.clip(drawn, min=-limit, max=limit).astype(held_as)


def setup_inputs(seed: int = 0) -> dict:
    keys = jax.random.split(jax.random.key(seed), 8)
    tokens = normal_values(keys[0], (TOKENS, D), 1.0, 6.0, ((0, 4),))
    routes_keys = jax.random.split(jax.random.fold_in(keys[1], 1), TOKENS // TOK_DP)
    routes_turns = jax.random.permutation(jax.random.fold_in(keys[1], 3), TOKENS // TOK_DP)
    routes = jax.vmap(lambda own, number: shared_out(jax.random.fold_in(keys[1], 2), own, number, TOK_DP, EXPERTS, TOP, CAP, 2))(routes_keys, routes_turns).reshape((TOKENS, TOP))
    route_weight = jnp.clip(jnp.exp(math.log(0.5) - 2.3025851 * jax.random.uniform(keys[2], (TOKENS, TOP), jnp.float32) ** block_scale(keys[2], (TOKENS, TOP), ((0, 4),), -0.2, 0.2)), 0.05, 0.5)
    w_gate = normal_values(keys[3], (EXPERTS * SHARDS, FF_DEV, D), D ** -0.5, 0.125, ((0, 32),))
    w_up = normal_values(keys[4], (EXPERTS * SHARDS, FF_DEV, D), D ** -0.5, 0.125, ((0, 32),))
    w_down = normal_values(keys[5], (EXPERTS * SHARDS, FF_DEV, D), FF ** -0.5, 0.15625, ((0, 32),))
    grad_out = normal_values(keys[6], (TOKENS, D), 1.0, 6.0, ((0, 32),))
    return {"tokens": tokens, "routes": routes, "route_weight": route_weight, "w_gate": w_gate, "w_up": w_up, "w_down": w_down, "grad_out": grad_out}


def silu_parts(gate_pre):
    sigma = jax.nn.sigmoid(gate_pre)
    return gate_pre * sigma, sigma * (1.0 + gate_pre * (1.0 - sigma))


def reference(tokens, routes, route_weight, w_gate, w_up, w_down, grad_out):
    tok_count, top_count = routes.shape
    width = tokens.shape[1]
    ff_dev = w_gate.shape[1]
    expert_count = w_gate.shape[0] // SHARDS
    hidden_width = ff_dev * SHARDS
    flat_routes = routes.reshape(-1)
    route_count = flat_routes.shape[0]
    most_rows = N_DP * CAP
    weights_flat = route_weight.reshape(-1)
    gate_all = w_gate.reshape(expert_count, hidden_width, width)
    up_all = w_up.reshape(expert_count, hidden_width, width)
    down_all = w_down.reshape(expert_count, hidden_width, width)

    def expert_step(carry, inputs):
        mixed_acc, dx_acc, grad_acc = carry
        expert_id, gate_matrix, up_matrix, down_matrix = inputs
        picked = jnp.nonzero(flat_routes == expert_id, size=most_rows, fill_value=route_count)[0].astype(jnp.int32)
        is_live = picked < route_count
        safe_index = jnp.where(is_live, picked, 0).astype(jnp.int32)
        token_of = (safe_index // top_count).astype(jnp.int32)
        x_rows = jnp.where(is_live[:, None], tokens[token_of], jnp.zeros((), tokens.dtype))
        gate_pre = jnp.dot(x_rows, gate_matrix.T, preferred_element_type=jnp.float32)
        up_pre = jnp.dot(x_rows, up_matrix.T, preferred_element_type=jnp.float32)
        silu_value, silu_slope = silu_parts(gate_pre)
        hidden = (silu_value * up_pre).astype(jnp.bfloat16)
        rows = hidden.shape[0]
        down_blocks = down_matrix.reshape(SHARDS, ff_dev, width).astype(jnp.float32)
        shard_part = jnp.einsum("rsf,sfd->rsd", hidden.reshape(rows, SHARDS, ff_dev).astype(jnp.float32), down_blocks).astype(jnp.bfloat16)
        weight_rows = jnp.where(is_live, weights_flat[safe_index], jnp.zeros((), weights_flat.dtype))
        part_sum = jnp.sum(shard_part.astype(jnp.float32), axis=1)
        mixed_acc = mixed_acc.at[token_of].add(weight_rows[:, None] * part_sum)
        cot_rows = grad_out[token_of]
        route_grad = jnp.sum(cot_rows.astype(jnp.float32)[:, None, :] * shard_part.astype(jnp.float32), axis=(1, 2))
        grad_acc = grad_acc.at[safe_index].add(jnp.where(is_live, route_grad, jnp.zeros((), route_grad.dtype)))
        route_cot = (weight_rows[:, None] * cot_rows.astype(jnp.float32)).astype(jnp.bfloat16)
        d_hidden = jnp.dot(route_cot, down_matrix.T, preferred_element_type=jnp.float32)
        d_gate = (d_hidden * up_pre * silu_slope).astype(jnp.bfloat16)
        d_up = (d_hidden * silu_value).astype(jnp.bfloat16)
        grad_down = jnp.dot(hidden.T, route_cot, preferred_element_type=jnp.float32).astype(jnp.bfloat16)
        grad_gate = jnp.dot(d_gate.T, x_rows, preferred_element_type=jnp.float32).astype(jnp.bfloat16)
        grad_up = jnp.dot(d_up.T, x_rows, preferred_element_type=jnp.float32).astype(jnp.bfloat16)
        gate_blocks = gate_matrix.reshape(SHARDS, ff_dev, width).astype(jnp.float32)
        up_blocks = up_matrix.reshape(SHARDS, ff_dev, width).astype(jnp.float32)
        shard_dx = jnp.einsum("rsf,sfd->rsd", d_gate.reshape(rows, SHARDS, ff_dev).astype(jnp.float32), gate_blocks)
        shard_dx = shard_dx + jnp.einsum("rsf,sfd->rsd", d_up.reshape(rows, SHARDS, ff_dev).astype(jnp.float32), up_blocks)
        shard_dx = shard_dx.astype(jnp.bfloat16)
        dx_sum = jnp.sum(shard_dx.astype(jnp.float32), axis=1)
        dx_acc = dx_acc.at[token_of].add(jnp.where(is_live[:, None], dx_sum, jnp.zeros((), dx_sum.dtype)))
        return (mixed_acc, dx_acc, grad_acc), (grad_gate, grad_up, grad_down)

    start = (jnp.zeros((tok_count, width), jnp.float32), jnp.zeros((tok_count, width), jnp.float32), jnp.zeros((route_count,), jnp.float32))
    carry, grads = lax.scan(expert_step, start, (jnp.arange(expert_count, dtype=jnp.int32), gate_all, up_all, down_all))
    mixed_acc, dx_acc, grad_acc = carry
    grad_gate = grads[0].reshape(expert_count * SHARDS, ff_dev, width)
    grad_up = grads[1].reshape(expert_count * SHARDS, ff_dev, width)
    grad_down = grads[2].reshape(expert_count * SHARDS, ff_dev, width)
    return (mixed_acc.astype(jnp.bfloat16), dx_acc.astype(jnp.bfloat16), grad_acc.reshape(tok_count, top_count), grad_gate, grad_up, grad_down)
```

```python
import jax
import jax.numpy as jnp
from jax import lax
from jax.experimental import pallas as pl
from jax.experimental.pallas import tpu as pltpu
from jax.sharding import PartitionSpec as P

SHARDS = 4
CORES = 2
LANES = 128
LEVEL_STEPS = (0, 2, 1, 3)
PACKED_ROWS = 16
VMEM_LIMIT = 32 * 1024 * 1024
GRADS_VMEM = 56 * 1024 * 1024


def silu_parts(gate_pre):
    sigma = jax.nn.sigmoid(gate_pre)
    return (gate_pre * sigma, sigma * (1.0 + gate_pre * (1.0 - sigma)))


def deliver(buffer):
    dp_count, slot_count, width = buffer.shape
    arrived = lax.all_to_all(buffer, "dp", split_axis=0, concat_axis=0, tiled=True)
    return arrived.reshape(dp_count * slot_count, width)


def send_back(rows, dp_count, slot_count):
    width = rows.shape[1]
    returned = lax.all_to_all(
        rows.reshape(dp_count, slot_count, width), "dp", split_axis=0, concat_axis=0, tiled=True
    )
    return (returned.reshape(dp_count * slot_count, width), jnp.zeros((), jnp.int32))


def padded_body(tokens, routes, route_weight, w_gate, w_up, w_down, grad_out):
    dp_count = lax.axis_size("dp")
    ex_count = lax.axis_size("expert")
    groups = ex_count // SHARDS
    my_group = lax.axis_index("expert") // SHARDS
    tok_rows, top_count = routes.shape
    width = tokens.shape[1]
    expert_count = dp_count * groups
    capacity = min(tok_rows, 3 * tok_rows * top_count // (2 * expert_count))
    flat_routes = routes.reshape(-1)
    route_count = flat_routes.shape[0]
    owner_ids = jnp.arange(dp_count, dtype=jnp.int32) * groups + my_group
    hit_table = (flat_routes[:, None] == owner_ids[None, :]).astype(jnp.int32)
    is_live = jnp.sum(hit_table, axis=1)
    owner_dp = jnp.sum(hit_table * jnp.arange(dp_count, dtype=jnp.int32)[None, :], axis=1)
    slot_index = jnp.sum((jnp.cumsum(hit_table, axis=0) - 1) * hit_table, axis=1)
    dump_row = dp_count * capacity
    target = jnp.where(is_live == 1, owner_dp * capacity + slot_index, dump_row)
    source = (
        jnp.full((dump_row + 1,), route_count, jnp.int32)
        .at[target]
        .set(jnp.arange(route_count, dtype=jnp.int32))[:dump_row]
    )
    filled = source < route_count
    safe_source = jnp.where(filled, source, 0)
    token_of = safe_source // top_count
    weights_flat = route_weight.reshape(-1)
    send_rows = jnp.where(filled[:, None], tokens[token_of], jnp.zeros((), tokens.dtype))
    x_rows = deliver(send_rows.reshape(dp_count, capacity, width))
    gate_matrix = w_gate[0]
    up_matrix = w_up[0]
    down_matrix = w_down[0]
    gate_pre = jnp.einsum("rd,fd->rf", x_rows, gate_matrix, preferred_element_type=jnp.float32)
    up_pre = jnp.einsum("rd,fd->rf", x_rows, up_matrix, preferred_element_type=jnp.float32)
    silu_value, silu_slope = silu_parts(gate_pre)
    hidden = (silu_value * up_pre).astype(jnp.bfloat16)
    shard_part = jnp.dot(hidden, down_matrix, preferred_element_type=jnp.float32).astype(
        jnp.bfloat16
    )
    returned, offset = send_back(shard_part, dp_count, capacity)
    piece_width = returned.shape[1]
    safe_target = jnp.where(is_live == 1, target, 0)
    route_part = jnp.where(
        is_live[:, None] == 1, returned[safe_target], jnp.zeros((), returned.dtype)
    )
    weighted = weights_flat[:, None] * route_part.astype(jnp.float32)
    mixed_part = jnp.sum(weighted.reshape(tok_rows, top_count, piece_width), axis=1)
    cotangent = lax.all_gather(grad_out, "expert", axis=0, tiled=True)
    route_grad = jnp.sum(
        route_part.reshape(tok_rows, top_count, piece_width).astype(jnp.float32)
        * cotangent[:, None, :].astype(jnp.float32),
        axis=2,
    )
    weight_of = jnp.where(filled, weights_flat[safe_source], jnp.zeros((), weights_flat.dtype))
    send_cot = (weight_of[:, None] * cotangent[token_of].astype(jnp.float32)).astype(jnp.bfloat16)
    cot_rows = deliver(send_cot.reshape(dp_count, capacity, width))
    d_hidden = jnp.einsum("rd,fd->rf", cot_rows, down_matrix, preferred_element_type=jnp.float32)
    d_gate = (d_hidden * up_pre * silu_slope).astype(jnp.bfloat16)
    d_up = (d_hidden * silu_value).astype(jnp.bfloat16)
    grad_down = jnp.einsum(
        "rf,rd->fd", hidden, cot_rows, preferred_element_type=jnp.float32
    ).astype(jnp.bfloat16)[None]
    grad_gate = jnp.einsum("rf,rd->fd", d_gate, x_rows, preferred_element_type=jnp.float32).astype(
        jnp.bfloat16
    )[None]
    grad_up = jnp.einsum("rf,rd->fd", d_up, x_rows, preferred_element_type=jnp.float32).astype(
        jnp.bfloat16
    )[None]
    shard_dx = jnp.dot(d_gate, gate_matrix, preferred_element_type=jnp.float32) + jnp.dot(
        d_up, up_matrix, preferred_element_type=jnp.float32
    )
    dx_back, dx_offset = send_back(shard_dx.astype(jnp.bfloat16), dp_count, capacity)
    route_dx = jnp.where(is_live[:, None] == 1, dx_back[safe_target], jnp.zeros((), dx_back.dtype))
    dx_part = jnp.sum(
        route_dx.astype(jnp.float32).reshape(tok_rows, top_count, piece_width), axis=1
    )
    mixed, grad_tokens, grad_route = (
        lax.psum_scatter(
            mixed_part.astype(jnp.bfloat16), "expert", scatter_dimension=0, tiled=True
        ).astype(jnp.float32),
        lax.psum_scatter(
            dx_part.astype(jnp.bfloat16), "expert", scatter_dimension=0, tiled=True
        ).astype(jnp.float32),
        lax.psum_scatter(
            route_grad.astype(jnp.bfloat16), "expert", scatter_dimension=0, tiled=True
        ).astype(jnp.float32),
    )
    return (
        mixed.astype(jnp.bfloat16),
        grad_tokens.astype(jnp.bfloat16),
        grad_route,
        grad_gate,
        grad_up,
        grad_down,
    )


FLOPS = 5_000_000_000
BYTES = 20_000_000


def dot_rows(left, right):
    return lax.dot_general(
        left, right, (((1,), (1,)), ((), ())), preferred_element_type=jnp.float32
    )


def dot_over_rows(left, right):
    return lax.dot_general(
        left, right, (((0,), (0,)), ((), ())), preferred_element_type=jnp.float32
    )


def padded(hidden_rows):
    return -(-hidden_rows // LANES) * LANES


def load_weights(refs, pre_buf, down_buf, sems):
    h = refs[0].shape[1]
    step = padded(h)
    copies = []
    for position, ref in enumerate(refs):
        buf, first = (pre_buf, position * step) if position < 4 else (down_buf, (position - 4) * step)
        copies.append(
            pltpu.make_async_copy(ref.at[0], buf.at[pl.ds(first, h)], sems.at[position])
        )
        if step > h:
            buf[first + h : first + step, :] = jnp.zeros((step - h, buf.shape[1]), buf.dtype)
    return copies


def load_rows(refs, buf, sems):
    rows = buf.shape[0] // len(refs)
    return [
        pltpu.make_async_copy(
            ref.at[pl.ds(0, rows)], buf.at[pl.ds(position * rows, rows)], sems.at[position]
        )
        for position, ref in enumerate(refs)
    ]


def forward_kernel(
    gate, gate_other, up, up_other, down, down_other, x_first, x_second, weight,
    mixed_out, hidden_out, weighted_out, to_gate_out, to_up_out,
    row_buf, pre_buf, down_buf, row_sems, sems,
):
    both = down_buf.shape[0]
    loads = load_weights(
        (gate, gate_other, up, up_other, down, down_other), pre_buf, down_buf, sems
    )
    loads += load_rows((x_first, x_second), row_buf, row_sems)
    for load in loads:
        load.start()
    for load in loads:
        load.wait()
    gate_pre = dot_rows(row_buf[...], pre_buf[:both])
    up_pre = dot_rows(row_buf[...], pre_buf[both:])
    silu_value, silu_slope = silu_parts(gate_pre)
    hidden = silu_value * up_pre
    weighted = (hidden * weight[...]).astype(jnp.bfloat16)
    hidden_out[...] = hidden.astype(jnp.bfloat16)
    weighted_out[...] = weighted
    to_gate_out[...] = up_pre * silu_slope
    to_up_out[...] = silu_value
    mixed_out[...] = jnp.dot(
        weighted, down_buf[...], preferred_element_type=jnp.float32
    ).astype(jnp.bfloat16)


def backward_kernel(
    gate, gate_other, up, up_other, down, down_other, cot_first, cot_second, weight,
    hidden, to_gate, to_up,
    dx_left, dx_right, route_out, d_gate_out, d_up_out,
    row_buf, pre_buf, down_buf, row_sems, sems,
):
    both = down_buf.shape[0]
    loads = load_weights(
        (gate, gate_other, up, up_other, down, down_other), pre_buf, down_buf, sems
    )
    first = load_rows((cot_first, cot_second), row_buf, row_sems) + loads[4:]
    for load in first + loads[:4]:
        load.start()
    for load in first:
        load.wait()
    plain = dot_rows(row_buf[...], down_buf[...])
    route_out[...] = jnp.sum(plain * hidden[...].astype(jnp.float32), axis=1, keepdims=True)
    d_hidden = plain * weight[...]
    d_gate = (d_hidden * to_gate[...]).astype(jnp.bfloat16)
    d_up = (d_hidden * to_up[...]).astype(jnp.bfloat16)
    d_gate_out[...] = d_gate
    d_up_out[...] = d_up
    for load in loads[:4]:
        load.wait()
    dx = jnp.dot(d_gate, pre_buf[:both], preferred_element_type=jnp.float32)
    dx = dx + jnp.dot(d_up, pre_buf[both:], preferred_element_type=jnp.float32)
    columns = dx_left.shape[1]
    dx_left[...] = dx[:, :columns].astype(jnp.bfloat16)
    dx_right[...] = dx[:, columns:].astype(jnp.bfloat16)


WIDE, NARROW = 8, 6


def weight_products(refs, first, count):
    xs, gs, narrow = refs[:4], refs[4:WIDE], refs[WIDE : WIDE + NARROW]
    rows = narrow[0].shape[0] // 2
    there = pl.ds(first, count)

    def product(pair, parts):
        total = None
        for position, part in enumerate(parts):
            here = pl.ds(position % 2 * rows, rows)
            term = dot_over_rows(pair[position // 2][here, there], part[...])
            total = term if total is None else total + term
        return total

    return product(narrow[0:2], xs), product(narrow[2:4], xs), product(narrow[4:6], gs)


def other_grads_kernel(*refs):
    out = refs[-1]
    count = refs[WIDE].shape[1] // 2
    h = out.shape[1]
    for position, product in enumerate(weight_products(refs, count, count)):
        out[position] = product[:h].astype(jnp.bfloat16)


def own_grads_kernel(*refs):
    received, outs = refs[WIDE + NARROW], refs[WIDE + NARROW + 1 :]
    count = refs[WIDE].shape[1] // 2
    h = received.shape[1]
    for position, product in enumerate(weight_products(refs, 0, count)):
        total = product[:h] + received[position].astype(jnp.float32)
        outs[position][0] = total.astype(jnp.bfloat16)


def cost():
    return pl.CostEstimate(flops=FLOPS, bytes_accessed=BYTES, transcendentals=0)


def specs(space, count):
    return [pl.BlockSpec(memory_space=space)] * count


def row_kernel(kernel, name, matrices, pair, operands, outs):
    _, h, width = matrices[0].shape
    step = padded(h)
    rows = operands[0].shape[0]
    return pl.pallas_call(
        kernel,
        out_shape=outs,
        in_specs=specs(pl.ANY, len(matrices) + 2) + specs(pltpu.VMEM, len(operands)),
        out_specs=specs(pltpu.VMEM, len(outs)),
        scratch_shapes=[
            pltpu.VMEM((rows, width), jnp.bfloat16),
            pltpu.VMEM((4 * step, width), jnp.bfloat16),
            pltpu.VMEM((2 * step, width), jnp.bfloat16),
            pltpu.SemaphoreType.DMA((2,)),
            pltpu.SemaphoreType.DMA((6,)),
        ],
        compiler_params=pltpu.CompilerParams(vmem_limit_bytes=VMEM_LIMIT),
        cost_estimate=cost(),
        name=name,
    )(*matrices, *pair, *operands)


def forward(matrices, pair, weight):
    rows, width = weight.shape[0], pair[0].shape[1]
    units = 2 * padded(matrices[0].shape[1])
    f32, bf16 = jnp.float32, jnp.bfloat16
    outs = [jax.ShapeDtypeStruct((rows, width), bf16)]
    outs += [jax.ShapeDtypeStruct((rows, units), kind) for kind in (bf16, bf16, f32, f32)]
    return row_kernel(forward_kernel, "forward", matrices, pair, (weight,), outs)


def backward(matrices, pair, weight, hidden, to_gate, to_up):
    rows, width = weight.shape[0], pair[0].shape[1]
    units = 2 * padded(matrices[0].shape[1])
    f32, bf16 = jnp.float32, jnp.bfloat16
    outs = [jax.ShapeDtypeStruct((rows, width // 2), bf16)] * 2
    outs += [jax.ShapeDtypeStruct((rows, 1), f32)]
    outs += [jax.ShapeDtypeStruct((rows, units), bf16)] * 2
    operands = (weight, hidden, to_gate, to_up)
    return row_kernel(backward_kernel, "backward", matrices, pair, operands, outs)


def weight_grads(wide, narrow, h, received=None):
    rows, width = narrow[0].shape[0] // 2, wide[0].shape[1]
    tile = min(512, width)
    tall = pl.BlockSpec((rows, tile), lambda n: (0, n))
    whole = pl.BlockSpec(narrow[0].shape, lambda n: (0, 0), pipeline_mode=pl.Buffered(1))
    three = pl.BlockSpec((3, h, tile), lambda n: (0, 0, n))
    in_specs = [tall] * len(wide) + [whole] * len(narrow)
    if received is None:
        kernel, more, name = other_grads_kernel, (), "other_grads"
        outs = jax.ShapeDtypeStruct((3, h, width), jnp.bfloat16)
        out_specs = three
    else:
        kernel, more, name = own_grads_kernel, (received,), "own_grads"
        outs = [jax.ShapeDtypeStruct((1, h, width), jnp.bfloat16)] * 3
        out_specs = [pl.BlockSpec((1, h, tile), lambda n: (0, 0, n))] * 3
        in_specs = in_specs + [three]
    return pl.pallas_call(
        kernel,
        out_shape=outs,
        grid=(width // tile,),
        in_specs=in_specs,
        out_specs=out_specs,
        compiler_params=pltpu.CompilerParams(vmem_limit_bytes=GRADS_VMEM),
        cost_estimate=cost(),
        name=name,
    )(*wide, *narrow, *more)


def all_slots_body(tokens, routes, route_weight, w_gate, w_up, w_down, grad_out):
    f32 = jnp.float32
    dp_count = lax.axis_size("dp")
    ex_count = lax.axis_size("expert")
    levels = ex_count // CORES
    groups = ex_count // SHARDS
    width = tokens.shape[1]
    block = grad_out.shape[0]
    half = levels * block
    dp_index = lax.axis_index("dp")
    ex_index = lax.axis_index("expert")
    level, core = ex_index // CORES, ex_index % CORES

    def pieces(values):
        rest, parts = values.reshape(-1), []
        for _ in range(3):
            part = lax.reduce_precision(rest, 8, 7)
            parts.append(part.astype(jnp.bfloat16))
            rest = rest - part
        row = jnp.concatenate(parts)
        row = jnp.pad(row, (0, PACKED_ROWS * width - row.shape[0]))
        return row.reshape(PACKED_ROWS, width)

    def whole(message, position):
        row = message[half : half + PACKED_ROWS].reshape(-1)[: 9 * half]
        parts = row.reshape(3, 3, half)[:, position].astype(f32)
        return (parts[0] + parts[1]) + parts[2]

    def exchange(value, partner):
        pairs = []
        for d in range(dp_count):
            for e in range(ex_count):
                other_d, other_e = partner(d, e // CORES, e % CORES)
                pairs.append((d * ex_count + e, other_d * ex_count + other_e))
        return lax.ppermute(value, ("dp", "expert"), pairs)

    def to_near(value):
        return exchange(value, lambda d, z, c: (d ^ (1 + c), z * CORES + c))

    def to_far(value):
        return exchange(value, lambda d, z, c: (d ^ (2 - c), z * CORES + c))

    def to_core(value):
        return exchange(value, lambda d, z, c: (d, z * CORES + 1 - c))

    def to_level(value, step):
        return exchange(value, lambda d, z, c: (d, (z ^ step) * CORES + c))

    def add(*terms):
        total = terms[0].astype(f32)
        for term in terms[1:]:
            total = total + term.astype(f32)
        return total.astype(terms[0].dtype)

    def after(value, *others):
        return lax.optimization_barrier((value, *others))[0]

    def by_halving(blocks):
        pair = add(blocks[:2], to_level(blocks[2:], 1))
        return add(pair[0], to_level(pair[1], 2))

    level_order = jnp.array(LEVEL_STEPS, jnp.int32) ^ level
    block_order = level_order * CORES + core
    near, far = dp_index ^ (1 + core), dp_index ^ (2 - core)
    group_dp = (dp_index, near, far, dp_index ^ 3)

    group_experts = jnp.arange(dp_count, dtype=jnp.int32) * groups + ex_index // SHARDS
    table = jnp.sum(
        jnp.where(routes[None] == group_experts[:, None, None], route_weight[None], 0.0), axis=2
    )
    table = table.reshape(dp_count, ex_count, block)[:, block_order]
    own_table, near_table, far_table, diagonal_table = (
        lax.dynamic_index_in_dim(table, d, axis=0).reshape(half) for d in group_dp
    )

    x_own = tokens.reshape(ex_count, block, width)[block_order].reshape(half, width)
    x_own = jnp.concatenate(
        [x_own, pieces(jnp.stack([near_table, far_table, diagonal_table]))], axis=0
    )
    x_near = to_near(x_own)
    x_far = to_far(x_own)
    others = [to_core(matrix) for matrix in (w_gate, w_up, w_down)]
    matrices = (w_gate, others[0], w_up, others[1], w_down, others[2])
    g_pair = jnp.concatenate([grad_out, to_level(grad_out, 2)], axis=0)
    x_last = to_far(x_near)
    weight12 = jnp.concatenate([own_table, whole(x_near, 0)])[:, None]
    weight34 = jnp.concatenate([whole(x_far, 1), whole(x_last, 2)])[:, None]

    mixed12, hidden12, weighted12, *slopes12 = forward(matrices, (x_own, x_near), weight12)
    x_last = after(x_last, mixed12)
    g_own = jnp.concatenate([g_pair, to_level(g_pair, 1)], axis=0)
    g_near = to_near(g_own)
    g_far = to_far(g_own)
    g_last = to_far(g_near)
    mixed34, hidden34, weighted34, *slopes34 = forward(matrices, (x_far, x_last), weight34)
    g_own, g_near = after((g_own, g_near), mixed34)
    *dx12, route12, gate12, up12 = backward(
        matrices, (g_own, g_near), weight12, hidden12, *slopes12
    )
    g_last = after(g_last, dx12)
    *dx34, route34, gate34, up34 = backward(
        matrices, (g_far, g_last), weight34, hidden34, *slopes34
    )

    mixed_sum = add(mixed12, after(to_far(after(mixed34, g_far)), dx34))
    mixed_near = to_near(mixed_sum[half:])
    mixed = add(mixed_sum[:half], mixed_near).reshape(levels, block, width)
    mixed = by_halving(mixed)

    h = w_gate.shape[1]
    wide = (x_own, x_near, x_far, x_last, g_own, g_near, g_far, g_last)
    narrow = (gate12, gate34, up12, up34, weighted12, weighted34)
    received = to_core(weight_grads(wide, narrow, h))
    grads = weight_grads(wide, narrow, h, received)

    route12 = route12.reshape(2, half)
    left_far = to_far(dx34[0])
    left_sum = add(dx12[0], left_far)
    left_near = to_near(after(left_sum[half:], mixed_near, *grads))
    right_far, route_far = lax.optimization_barrier(
        (to_far(after(dx34[1], left_far)), to_far(route34.reshape(2, half)))
    )
    right_sum = add(dx12[1], right_far)
    right_near = to_near(after(right_sum[half:], left_near))
    route_near = to_near(jnp.stack([route12[1], route_far[1]]))

    left_near = after(left_near, right_sum)
    left = add(left_sum[:half], left_near).reshape(levels, block, width // 2)
    left = by_halving(left)
    right_near, route_near, *_ = lax.optimization_barrier((right_near, route_near, mixed))
    right = add(right_sum[:half], right_near).reshape(levels, block, width // 2)
    right = [right[0]] + [
        to_level(right[k], step) for k, step in enumerate(LEVEL_STEPS) if k > 0
    ]
    right = add(*right)
    grad_tokens = jnp.concatenate([left, right], axis=1)

    route_own = jnp.stack([route12[0], route_far[0], route_near[0], route_near[1]])
    route_own = route_own.reshape(dp_count, levels, block)
    route_own = route_own[:, :2] + to_level(route_own[:, 2:], 1)
    by_group = (route_own[:, 0], to_level(route_own[:, 1], 2))
    my_routes = lax.dynamic_slice_in_dim(routes, ex_index * block, block, axis=0)
    my_group = ex_index // SHARDS
    grad_route = jnp.zeros(my_routes.shape, f32)
    for values, group in zip(by_group, (my_group, 1 - my_group)):
        for position, d in enumerate((dp_index, far, near, dp_index ^ 3)):
            grad_route = grad_route + jnp.where(
                my_routes == d * groups + group, values[position][:, None], 0.0
            )
    return (mixed, grad_tokens, grad_route, *grads)


def body(tokens, routes, *rest):
    dp_count = lax.axis_size("dp")
    ex_count = lax.axis_size("expert")
    tok_rows, top_count = routes.shape
    expert_count = dp_count * ex_count // SHARDS
    every_slot = 3 * tok_rows * top_count >= 2 * expert_count * tok_rows
    if every_slot and dp_count == 4 and ex_count == CORES * len(LEVEL_STEPS):
        return all_slots_body(tokens, routes, *rest)
    return padded_body(tokens, routes, *rest)


def solution(mesh):
    return jax.shard_map(
        body,
        mesh=mesh,
        in_specs=(
            P("dp", None),
            P("dp", None),
            P("dp", None),
            P(("dp", "expert"), None, None),
            P(("dp", "expert"), None, None),
            P(("dp", "expert"), None, None),
            P(("dp", "expert"), None),
        ),
        out_specs=(
            P(("dp", "expert"), None),
            P(("dp", "expert"), None),
            P(("dp", "expert"), None),
            P(("dp", "expert"), None, None),
            P(("dp", "expert"), None, None),
            P(("dp", "expert"), None, None),
        ),
        check_vma=False,
    )
```

```python
import jax
import jax.numpy as jnp
from jax import lax
from jax.experimental import pallas as pl
from jax.experimental.pallas import tpu as pltpu
from jax.sharding import PartitionSpec as P

SHARDS = 4
CORES = 2
LANES = 128
UNIT_TILE = 256
COLUMN_TILE = 512
LEVEL_STEPS = (0, 2, 1, 3)
PACKED_ROWS = 16
VMEM_LIMIT = 56 * 1024 * 1024


def silu_parts(gate_pre):
    sigma = jax.nn.sigmoid(gate_pre)
    return (gate_pre * sigma, sigma * (1.0 + gate_pre * (1.0 - sigma)))


def deliver(buffer):
    dp_count, slot_count, width = buffer.shape
    arrived = lax.all_to_all(buffer, "dp", split_axis=0, concat_axis=0, tiled=True)
    return arrived.reshape(dp_count * slot_count, width)


def send_back(rows, dp_count, slot_count):
    width = rows.shape[1]
    returned = lax.all_to_all(
        rows.reshape(dp_count, slot_count, width), "dp", split_axis=0, concat_axis=0, tiled=True
    )
    return (returned.reshape(dp_count * slot_count, width), jnp.zeros((), jnp.int32))


def padded_body(tokens, routes, route_weight, w_gate, w_up, w_down, grad_out):
    dp_count = lax.axis_size("dp")
    ex_count = lax.axis_size("expert")
    groups = ex_count // SHARDS
    my_group = lax.axis_index("expert") // SHARDS
    tok_rows, top_count = routes.shape
    width = tokens.shape[1]
    expert_count = dp_count * groups
    capacity = min(tok_rows, 3 * tok_rows * top_count // (2 * expert_count))
    flat_routes = routes.reshape(-1)
    route_count = flat_routes.shape[0]
    owner_ids = jnp.arange(dp_count, dtype=jnp.int32) * groups + my_group
    hit_table = (flat_routes[:, None] == owner_ids[None, :]).astype(jnp.int32)
    is_live = jnp.sum(hit_table, axis=1)
    owner_dp = jnp.sum(hit_table * jnp.arange(dp_count, dtype=jnp.int32)[None, :], axis=1)
    slot_index = jnp.sum((jnp.cumsum(hit_table, axis=0) - 1) * hit_table, axis=1)
    dump_row = dp_count * capacity
    target = jnp.where(is_live == 1, owner_dp * capacity + slot_index, dump_row)
    source = (
        jnp.full((dump_row + 1,), route_count, jnp.int32)
        .at[target]
        .set(jnp.arange(route_count, dtype=jnp.int32))[:dump_row]
    )
    filled = source < route_count
    safe_source = jnp.where(filled, source, 0)
    token_of = safe_source // top_count
    weights_flat = route_weight.reshape(-1)
    send_rows = jnp.where(filled[:, None], tokens[token_of], jnp.zeros((), tokens.dtype))
    x_rows = deliver(send_rows.reshape(dp_count, capacity, width))
    gate_matrix = w_gate[0]
    up_matrix = w_up[0]
    down_matrix = w_down[0]
    gate_pre = jnp.einsum("rd,fd->rf", x_rows, gate_matrix, preferred_element_type=jnp.float32)
    up_pre = jnp.einsum("rd,fd->rf", x_rows, up_matrix, preferred_element_type=jnp.float32)
    silu_value, silu_slope = silu_parts(gate_pre)
    hidden = (silu_value * up_pre).astype(jnp.bfloat16)
    shard_part = jnp.dot(hidden, down_matrix, preferred_element_type=jnp.float32).astype(
        jnp.bfloat16
    )
    returned, offset = send_back(shard_part, dp_count, capacity)
    piece_width = returned.shape[1]
    safe_target = jnp.where(is_live == 1, target, 0)
    route_part = jnp.where(
        is_live[:, None] == 1, returned[safe_target], jnp.zeros((), returned.dtype)
    )
    weighted = weights_flat[:, None] * route_part.astype(jnp.float32)
    mixed_part = jnp.sum(weighted.reshape(tok_rows, top_count, piece_width), axis=1)
    cotangent = lax.all_gather(grad_out, "expert", axis=0, tiled=True)
    route_grad = jnp.sum(
        route_part.reshape(tok_rows, top_count, piece_width).astype(jnp.float32)
        * cotangent[:, None, :].astype(jnp.float32),
        axis=2,
    )
    weight_of = jnp.where(filled, weights_flat[safe_source], jnp.zeros((), weights_flat.dtype))
    send_cot = (weight_of[:, None] * cotangent[token_of].astype(jnp.float32)).astype(jnp.bfloat16)
    cot_rows = deliver(send_cot.reshape(dp_count, capacity, width))
    d_hidden = jnp.einsum("rd,fd->rf", cot_rows, down_matrix, preferred_element_type=jnp.float32)
    d_gate = (d_hidden * up_pre * silu_slope).astype(jnp.bfloat16)
    d_up = (d_hidden * silu_value).astype(jnp.bfloat16)
    grad_down = jnp.einsum(
        "rf,rd->fd", hidden, cot_rows, preferred_element_type=jnp.float32
    ).astype(jnp.bfloat16)[None]
    grad_gate = jnp.einsum("rf,rd->fd", d_gate, x_rows, preferred_element_type=jnp.float32).astype(
        jnp.bfloat16
    )[None]
    grad_up = jnp.einsum("rf,rd->fd", d_up, x_rows, preferred_element_type=jnp.float32).astype(
        jnp.bfloat16
    )[None]
    shard_dx = jnp.dot(d_gate, gate_matrix, preferred_element_type=jnp.float32) + jnp.dot(
        d_up, up_matrix, preferred_element_type=jnp.float32
    )
    dx_back, dx_offset = send_back(shard_dx.astype(jnp.bfloat16), dp_count, capacity)
    route_dx = jnp.where(is_live[:, None] == 1, dx_back[safe_target], jnp.zeros((), dx_back.dtype))
    dx_part = jnp.sum(
        route_dx.astype(jnp.float32).reshape(tok_rows, top_count, piece_width), axis=1
    )
    mixed, grad_tokens, grad_route = (
        lax.psum_scatter(
            mixed_part.astype(jnp.bfloat16), "expert", scatter_dimension=0, tiled=True
        ).astype(jnp.float32),
        lax.psum_scatter(
            dx_part.astype(jnp.bfloat16), "expert", scatter_dimension=0, tiled=True
        ).astype(jnp.float32),
        lax.psum_scatter(
            route_grad.astype(jnp.bfloat16), "expert", scatter_dimension=0, tiled=True
        ).astype(jnp.float32),
    )
    return (
        mixed.astype(jnp.bfloat16),
        grad_tokens.astype(jnp.bfloat16),
        grad_route,
        grad_gate,
        grad_up,
        grad_down,
    )


FLOPS = 5_000_000_000
BYTES = 20_000_000


def dot_rows(left, right):
    return lax.dot_general(
        left, right, (((1,), (1,)), ((), ())), preferred_element_type=jnp.float32
    )


def dot_over_rows(left, right):
    return lax.dot_general(
        left, right, (((0,), (0,)), ((), ())), preferred_element_type=jnp.float32
    )


def padded(hidden_rows):
    return -(-hidden_rows // LANES) * LANES


def load_weights(refs, pre_buf, down_buf, sems):
    h = refs[0].shape[1]
    step = padded(h)
    copies = []
    for position, ref in enumerate(refs):
        buf, first = (pre_buf, position * step) if position < 4 else (down_buf, (position - 4) * step)
        copies.append(
            pltpu.make_async_copy(ref.at[0], buf.at[pl.ds(first, h)], sems.at[position])
        )
        if step > h:
            buf[first + h : first + step, :] = jnp.zeros((step - h, buf.shape[1]), buf.dtype)
    return copies


def dot_columns(out, left, right):
    for first in range(0, out.shape[1], COLUMN_TILE):
        there = pl.ds(first, min(COLUMN_TILE, out.shape[1] - first))
        out[:, there] = jnp.dot(
            left[...], right[:, there], preferred_element_type=jnp.float32
        ).astype(out.dtype)


def load_rows(refs, buf, sems):
    rows = buf.shape[0] // len(refs)
    return [
        pltpu.make_async_copy(
            ref.at[pl.ds(0, rows)], buf.at[pl.ds(position * rows, rows)], sems.at[position]
        )
        for position, ref in enumerate(refs)
    ]


def start(copies):
    for copy in copies:
        copy.start()


def wait(copies):
    for copy in copies:
        copy.wait()


def copies_between(pairs, sems):
    return [
        pltpu.make_async_copy(source, place, sems.at[position])
        for position, (source, place) in enumerate(pairs)
    ]


def forward_kernel(
    gate, gate_other, up, up_other, down, down_other, x_first, x_second, weight,
    mixed_out, hidden_out, weighted_out, to_gate_out, to_up_out,
    row_buf, pre_buf, down_buf, mixed, hidden, weighted, to_gate, to_up,
    row_sems, sems, out_sems,
):
    both = down_buf.shape[0]
    loads = load_weights(
        (gate, gate_other, up, up_other, down, down_other), pre_buf, down_buf, sems
    )
    rows = load_rows((x_first, x_second), row_buf, row_sems)
    stores = copies_between(
        (
            (hidden, hidden_out),
            (weighted, weighted_out),
            (to_gate, to_gate_out),
            (to_up, to_up_out),
            (mixed, mixed_out),
        ),
        out_sems,
    )
    start(rows + loads)
    wait(rows + loads[:4])
    for first in range(0, both, UNIT_TILE):
        there = pl.ds(first, UNIT_TILE)
        gate_pre = dot_rows(row_buf[...], pre_buf[there])
        up_pre = dot_rows(row_buf[...], pre_buf[pl.ds(both + first, UNIT_TILE)])
        silu_value, silu_slope = silu_parts(gate_pre)
        product = silu_value * up_pre
        hidden[:, there] = product.astype(jnp.bfloat16)
        weighted[:, there] = (product * weight[...]).astype(jnp.bfloat16)
        to_gate[:, there] = up_pre * silu_slope
        to_up[:, there] = silu_value
    start(stores[:4])
    wait(loads[4:])
    dot_columns(mixed, weighted, down_buf)
    start(stores[4:])
    wait(stores)


def backward_kernel(
    gate, gate_other, up, up_other, down, down_other, cot_first, cot_second, weight,
    hidden_in, to_gate_in, to_up_in,
    dx_out, route_out, d_gate_out, d_up_out,
    row_buf, pre_buf, down_buf, dx, d_pre, hidden, to_gate, to_up,
    row_sems, sems, in_sems, out_sems,
):
    both = down_buf.shape[0]
    loads = load_weights(
        (gate, gate_other, up, up_other, down, down_other), pre_buf, down_buf, sems
    )
    rows = load_rows((cot_first, cot_second), row_buf, row_sems)
    parts = copies_between(
        ((hidden_in, hidden), (to_gate_in, to_gate), (to_up_in, to_up)), in_sems
    )
    stores = copies_between(
        (
            (d_pre.at[:, pl.ds(0, both)], d_gate_out),
            (d_pre.at[:, pl.ds(both, both)], d_up_out),
            (dx, dx_out),
        ),
        out_sems,
    )
    start(rows + loads[4:] + parts + loads[:4])
    wait(rows + loads[4:] + parts)
    route = None
    for first in range(0, both, UNIT_TILE):
        there = pl.ds(first, UNIT_TILE)
        plain = dot_rows(row_buf[...], down_buf[there])
        term = jnp.sum(plain * hidden[:, there].astype(jnp.float32), axis=1, keepdims=True)
        route = term if route is None else route + term
        d_hidden = plain * weight[...]
        d_pre[:, there] = (d_hidden * to_gate[:, there]).astype(jnp.bfloat16)
        d_pre[:, pl.ds(both + first, UNIT_TILE)] = (d_hidden * to_up[:, there]).astype(jnp.bfloat16)
    route_out[...] = route
    start(stores[:2])
    wait(loads[:4])
    dot_columns(dx, d_pre, pre_buf)
    start(stores[2:])
    wait(stores)


WIDE, NARROW = 8, 6


def weight_products(refs, first, count):
    xs, gs, narrow = refs[:4], refs[4:WIDE], refs[WIDE : WIDE + NARROW]
    rows = narrow[0].shape[0] // 2
    there = pl.ds(first, count)

    def product(pair, parts):
        total = None
        for position, part in enumerate(parts):
            here = pl.ds(position % 2 * rows, rows)
            term = dot_over_rows(pair[position // 2][here, there], part[...])
            total = term if total is None else total + term
        return total

    return product(narrow[0:2], xs), product(narrow[2:4], xs), product(narrow[4:6], gs)


def other_grads_kernel(*refs):
    out = refs[-1]
    count = refs[WIDE].shape[1] // 2
    h = out.shape[1]
    for position, product in enumerate(weight_products(refs, count, count)):
        out[position] = product[:h].astype(jnp.bfloat16)


def own_grads_kernel(*refs):
    received, outs = refs[WIDE + NARROW], refs[WIDE + NARROW + 1 :]
    count = refs[WIDE].shape[1] // 2
    h = received.shape[1]
    for position, product in enumerate(weight_products(refs, 0, count)):
        total = product[:h] + received[position].astype(jnp.float32)
        outs[position][0] = total.astype(jnp.bfloat16)


def cost():
    return pl.CostEstimate(flops=FLOPS, bytes_accessed=BYTES, transcendentals=0)


def specs(space, count):
    return [pl.BlockSpec(memory_space=space)] * count


def row_kernel(kernel, name, matrices, pair, weight, parts, outs, in_vmem, buffers, copied):
    _, h, width = matrices[0].shape
    step = padded(h)
    rows = weight.shape[0]
    sems = [2, 6] + [len(parts)] * bool(parts) + [copied]
    space = [pltpu.VMEM if position in in_vmem else pl.ANY for position in range(len(outs))]
    return pl.pallas_call(
        kernel,
        out_shape=outs,
        in_specs=specs(pl.ANY, len(matrices) + 2)
        + specs(pltpu.VMEM, 1)
        + specs(pl.ANY, len(parts)),
        out_specs=[pl.BlockSpec(memory_space=kind) for kind in space],
        scratch_shapes=[
            pltpu.VMEM((rows, width), jnp.bfloat16),
            pltpu.VMEM((4 * step, width), jnp.bfloat16),
            pltpu.VMEM((2 * step, width), jnp.bfloat16),
            *[
                pltpu.VMEM(array.shape, array.dtype)
                for array in (*buffers, *parts)
            ],
            *[pltpu.SemaphoreType.DMA((count,)) for count in sems],
        ],
        compiler_params=pltpu.CompilerParams(vmem_limit_bytes=VMEM_LIMIT),
        cost_estimate=cost(),
        name=name,
    )(*matrices, *pair, weight, *parts)


def forward(matrices, pair, weight):
    rows, width = weight.shape[0], pair[0].shape[1]
    units = 2 * padded(matrices[0].shape[1])
    f32, bf16 = jnp.float32, jnp.bfloat16
    outs = [jax.ShapeDtypeStruct((rows, width), bf16)]
    outs += [jax.ShapeDtypeStruct((rows, units), kind) for kind in (bf16, bf16, f32, f32)]
    return row_kernel(forward_kernel, "forward", matrices, pair, weight, (), outs, (), outs, 5)


def backward(matrices, pair, weight, hidden, to_gate, to_up):
    rows, width = weight.shape[0], pair[0].shape[1]
    units = 2 * padded(matrices[0].shape[1])
    f32, bf16 = jnp.float32, jnp.bfloat16
    outs = [jax.ShapeDtypeStruct((rows, width), bf16), jax.ShapeDtypeStruct((rows, 1), f32)]
    outs += [jax.ShapeDtypeStruct((rows, units), bf16)] * 2
    parts = (hidden, to_gate, to_up)
    buffers = (outs[0], jax.ShapeDtypeStruct((rows, 2 * units), bf16))
    return row_kernel(
        backward_kernel, "backward", matrices, pair, weight, parts, outs, (1,), buffers, 3
    )


def weight_grads(wide, narrow, h, received=None):
    rows, width = narrow[0].shape[0] // 2, wide[0].shape[1]
    tile = min(512, width)
    tall = pl.BlockSpec((rows, tile), lambda n: (0, n))
    whole = pl.BlockSpec(narrow[0].shape, lambda n: (0, 0), pipeline_mode=pl.Buffered(1))
    three = pl.BlockSpec((3, h, tile), lambda n: (0, 0, n))
    in_specs = [tall] * len(wide) + [whole] * len(narrow)
    if received is None:
        kernel, more, name = other_grads_kernel, (), "other_grads"
        outs = jax.ShapeDtypeStruct((3, h, width), jnp.bfloat16)
        out_specs = three
    else:
        kernel, more, name = own_grads_kernel, (received,), "own_grads"
        outs = [jax.ShapeDtypeStruct((1, h, width), jnp.bfloat16)] * 3
        out_specs = [pl.BlockSpec((1, h, tile), lambda n: (0, 0, n))] * 3
        in_specs = in_specs + [three]
    return pl.pallas_call(
        kernel,
        out_shape=outs,
        grid=(width // tile,),
        in_specs=in_specs,
        out_specs=out_specs,
        compiler_params=pltpu.CompilerParams(vmem_limit_bytes=VMEM_LIMIT),
        cost_estimate=cost(),
        name=name,
    )(*wide, *narrow, *more)


def all_slots_body(tokens, routes, route_weight, w_gate, w_up, w_down, grad_out):
    f32 = jnp.float32
    dp_count = lax.axis_size("dp")
    ex_count = lax.axis_size("expert")
    levels = ex_count // CORES
    groups = ex_count // SHARDS
    width = tokens.shape[1]
    block = grad_out.shape[0]
    half = levels * block
    dp_index = lax.axis_index("dp")
    ex_index = lax.axis_index("expert")
    level, core = ex_index // CORES, ex_index % CORES

    def pieces(values):
        rest, parts = values.reshape(-1), []
        for _ in range(3):
            part = lax.reduce_precision(rest, 8, 7)
            parts.append(part.astype(jnp.bfloat16))
            rest = rest - part
        row = jnp.concatenate(parts)
        row = jnp.pad(row, (0, PACKED_ROWS * width - row.shape[0]))
        return row.reshape(PACKED_ROWS, width)

    def whole(message, position):
        row = message[half : half + PACKED_ROWS].reshape(-1)[: 9 * half]
        parts = row.reshape(3, 3, half)[:, position].astype(f32)
        return (parts[0] + parts[1]) + parts[2]

    def exchange(value, partner):
        pairs = []
        for d in range(dp_count):
            for e in range(ex_count):
                other_d, other_e = partner(d, e // CORES, e % CORES)
                pairs.append((d * ex_count + e, other_d * ex_count + other_e))
        return lax.ppermute(value, ("dp", "expert"), pairs)

    def to_near(value):
        return exchange(value, lambda d, z, c: (d ^ (1 + c), z * CORES + c))

    def to_far(value):
        return exchange(value, lambda d, z, c: (d ^ (2 - c), z * CORES + c))

    def to_core(value):
        return exchange(value, lambda d, z, c: (d, z * CORES + 1 - c))

    def to_level(value, step):
        return exchange(value, lambda d, z, c: (d, (z ^ step) * CORES + c))

    def add(*terms):
        total = terms[0].astype(f32)
        for term in terms[1:]:
            total = total + term.astype(f32)
        return total.astype(terms[0].dtype)

    def after(value, *others):
        return lax.optimization_barrier((value, *others))[0]

    def in_blocks(terms):
        return [term.reshape(levels, block, term.shape[-1]) for term in terms]

    def by_blocks(terms, *wait_for):
        terms = in_blocks(terms)
        received = [
            to_level(add(*[term[k] for term in terms]), step)
            for k, step in enumerate(LEVEL_STEPS)
            if k > 0
        ]
        own = after(terms[0][0], *wait_for)
        return add(own, *[term[0] for term in terms[1:]], *received)

    level_order = jnp.array(LEVEL_STEPS, jnp.int32) ^ level
    block_order = level_order * CORES + core
    near, far = dp_index ^ (1 + core), dp_index ^ (2 - core)
    group_dp = (dp_index, near, far, dp_index ^ 3)

    group_experts = jnp.arange(dp_count, dtype=jnp.int32) * groups + ex_index // SHARDS
    table = jnp.sum(
        jnp.where(routes[None] == group_experts[:, None, None], route_weight[None], 0.0), axis=2
    )
    table = table.reshape(dp_count, ex_count, block)[:, block_order]
    own_table, near_table, far_table, diagonal_table = (
        lax.dynamic_index_in_dim(table, d, axis=0).reshape(half) for d in group_dp
    )

    x_own = tokens.reshape(ex_count, block, width)[block_order].reshape(half, width)
    x_own = jnp.concatenate(
        [x_own, pieces(jnp.stack([near_table, far_table, diagonal_table]))], axis=0
    )
    x_near = to_near(x_own)
    x_far = to_far(x_own)
    others = [to_core(matrix) for matrix in (w_gate, w_up, w_down)]
    matrices = (w_gate, others[0], w_up, others[1], w_down, others[2])
    cotangent = after(grad_out, x_own)
    g_pair = jnp.concatenate([cotangent, to_level(cotangent, 2)], axis=0)
    x_last = to_far(after(x_near, x_far))
    weight12 = jnp.concatenate([own_table, whole(x_near, 0)])[:, None]
    weight34 = jnp.concatenate([whole(x_far, 1), whole(x_last, 2)])[:, None]

    mixed12, hidden12, weighted12, *slopes12 = forward(matrices, (x_own, x_near), weight12)
    x_last = after(x_last, mixed12)
    g_own = jnp.concatenate([g_pair, to_level(g_pair, 1)], axis=0)
    g_own = after(g_own, x_near, x_far)
    g_near = to_near(g_own)
    g_far = to_far(after(g_own, x_last, g_near))
    g_last = to_far(after(g_near, x_last))
    dx12, route12, gate12, up12 = backward(
        matrices, after((g_own, g_near), x_last), weight12, hidden12, *slopes12
    )
    x_far, x_last = after((x_far, x_last), dx12)
    mixed34, hidden34, weighted34, *slopes34 = forward(matrices, (x_far, x_last), weight34)
    g_last = after(g_last, mixed34)
    dx34, route34, gate34, up34 = backward(
        matrices, (g_far, g_last), weight34, hidden34, *slopes34
    )

    mixed_far = to_far(after(mixed34, g_far, g_last))
    mixed_part = add(mixed12[half:], after(mixed_far, dx34)[half:])
    mixed_near = to_near(mixed_part)

    mixed_terms = in_blocks((mixed12[:half], mixed_far[:half], mixed_near))
    mixed_pair = add(*[term[2:] for term in mixed_terms])
    dx_far = to_far(dx34)
    dx_part = add(dx12[half:], after(dx_far, mixed_pair)[half:])
    dx_near = to_near(dx_part)
    mixed_pair = after(to_level(mixed_pair, 1), dx_part)
    mixed_last = to_level(add(*[term[1] for term in mixed_terms], mixed_pair[1]), 2)

    h = w_gate.shape[1]
    wide = (x_own, x_near, x_far, x_last, g_own, g_near, g_far, g_last)
    narrow = after((gate12, gate34, up12, up34, weighted12, weighted34), mixed_far)
    received = to_core(weight_grads(wide, narrow, h))
    grads = weight_grads(wide, narrow, h, received)

    route = jnp.concatenate([route12, route34]).reshape(dp_count, levels, block)
    pair = after(to_level(route[:, 2:], 1), mixed_part)
    other_group = after(to_level(route[:, 1] + pair[:, 1], 2), mixed_near)
    route = jnp.stack([route[:, 0] + pair[:, 0], other_group], axis=1)
    route_far = after(to_far(route[2:]), dx_near)
    route_near = to_near(jnp.stack([route[1], route_far[1]]))

    mixed_last = after(mixed_last, *grads)
    mixed = add(*[term[0] for term in mixed_terms], mixed_pair[0], mixed_last)
    grad_tokens = by_blocks((dx12[:half], dx_far[:half], dx_near), *grads)

    route_own = jnp.stack([route[0], route_far[0], route_near[0], route_near[1]])
    my_routes = lax.dynamic_slice_in_dim(routes, ex_index * block, block, axis=0)
    my_group = ex_index // SHARDS
    grad_route = jnp.zeros(my_routes.shape, f32)
    for which, group in enumerate((my_group, 1 - my_group)):
        for position, d in enumerate((dp_index, far, near, dp_index ^ 3)):
            grad_route = grad_route + jnp.where(
                my_routes == d * groups + group, route_own[position, which][:, None], 0.0
            )
    return (mixed, grad_tokens, grad_route, *grads)


def body(tokens, routes, *rest):
    dp_count = lax.axis_size("dp")
    ex_count = lax.axis_size("expert")
    tok_rows, top_count = routes.shape
    expert_count = dp_count * ex_count // SHARDS
    every_slot = 3 * tok_rows * top_count >= 2 * expert_count * tok_rows
    if every_slot and dp_count == 4 and ex_count == CORES * len(LEVEL_STEPS):
        return all_slots_body(tokens, routes, *rest)
    return padded_body(tokens, routes, *rest)


def solution(mesh):
    return jax.shard_map(
        body,
        mesh=mesh,
        in_specs=(
            P("dp", None),
            P("dp", None),
            P("dp", None),
            P(("dp", "expert"), None, None),
            P(("dp", "expert"), None, None),
            P(("dp", "expert"), None, None),
            P(("dp", "expert"), None),
        ),
        out_specs=(
            P(("dp", "expert"), None),
            P(("dp", "expert"), None),
            P(("dp", "expert"), None),
            P(("dp", "expert"), None, None),
            P(("dp", "expert"), None, None),
            P(("dp", "expert"), None, None),
        ),
        check_vma=False,
    )
```

```python
import jax
import jax.numpy as jnp
from jax import lax
from jax.experimental import pallas as pl
from jax.experimental.pallas import tpu as pltpu
from jax.sharding import PartitionSpec as P

SHARDS = 4
CORES = 2
LANES = 128
UNIT_TILE = 256
COLUMN_TILE = 512
LEVEL_STEPS = (0, 2, 1, 3)
PACKED_ROWS = 16
VMEM_LIMIT = 56 * 1024 * 1024


def silu_parts(gate_pre):
    sigma = jax.nn.sigmoid(gate_pre)
    return (gate_pre * sigma, sigma * (1.0 + gate_pre * (1.0 - sigma)))


def deliver(buffer):
    dp_count, slot_count, width = buffer.shape
    arrived = lax.all_to_all(buffer, "dp", split_axis=0, concat_axis=0, tiled=True)
    return arrived.reshape(dp_count * slot_count, width)


def send_back(rows, dp_count, slot_count):
    width = rows.shape[1]
    returned = lax.all_to_all(
        rows.reshape(dp_count, slot_count, width), "dp", split_axis=0, concat_axis=0, tiled=True
    )
    return (returned.reshape(dp_count * slot_count, width), jnp.zeros((), jnp.int32))


def padded_body(tokens, routes, route_weight, w_gate, w_up, w_down, grad_out):
    dp_count = lax.axis_size("dp")
    ex_count = lax.axis_size("expert")
    groups = ex_count // SHARDS
    my_group = lax.axis_index("expert") // SHARDS
    tok_rows, top_count = routes.shape
    width = tokens.shape[1]
    expert_count = dp_count * groups
    capacity = min(tok_rows, 3 * tok_rows * top_count // (2 * expert_count))
    flat_routes = routes.reshape(-1)
    route_count = flat_routes.shape[0]
    owner_ids = jnp.arange(dp_count, dtype=jnp.int32) * groups + my_group
    hit_table = (flat_routes[:, None] == owner_ids[None, :]).astype(jnp.int32)
    is_live = jnp.sum(hit_table, axis=1)
    owner_dp = jnp.sum(hit_table * jnp.arange(dp_count, dtype=jnp.int32)[None, :], axis=1)
    slot_index = jnp.sum((jnp.cumsum(hit_table, axis=0) - 1) * hit_table, axis=1)
    dump_row = dp_count * capacity
    target = jnp.where(is_live == 1, owner_dp * capacity + slot_index, dump_row)
    source = (
        jnp.full((dump_row + 1,), route_count, jnp.int32)
        .at[target]
        .set(jnp.arange(route_count, dtype=jnp.int32))[:dump_row]
    )
    filled = source < route_count
    safe_source = jnp.where(filled, source, 0)
    token_of = safe_source // top_count
    weights_flat = route_weight.reshape(-1)
    send_rows = jnp.where(filled[:, None], tokens[token_of], jnp.zeros((), tokens.dtype))
    x_rows = deliver(send_rows.reshape(dp_count, capacity, width))
    gate_matrix = w_gate[0]
    up_matrix = w_up[0]
    down_matrix = w_down[0]
    gate_pre = jnp.einsum("rd,fd->rf", x_rows, gate_matrix, preferred_element_type=jnp.float32)
    up_pre = jnp.einsum("rd,fd->rf", x_rows, up_matrix, preferred_element_type=jnp.float32)
    silu_value, silu_slope = silu_parts(gate_pre)
    hidden = (silu_value * up_pre).astype(jnp.bfloat16)
    shard_part = jnp.dot(hidden, down_matrix, preferred_element_type=jnp.float32).astype(
        jnp.bfloat16
    )
    returned, offset = send_back(shard_part, dp_count, capacity)
    piece_width = returned.shape[1]
    safe_target = jnp.where(is_live == 1, target, 0)
    route_part = jnp.where(
        is_live[:, None] == 1, returned[safe_target], jnp.zeros((), returned.dtype)
    )
    weighted = weights_flat[:, None] * route_part.astype(jnp.float32)
    mixed_part = jnp.sum(weighted.reshape(tok_rows, top_count, piece_width), axis=1)
    cotangent = lax.all_gather(grad_out, "expert", axis=0, tiled=True)
    route_grad = jnp.sum(
        route_part.reshape(tok_rows, top_count, piece_width).astype(jnp.float32)
        * cotangent[:, None, :].astype(jnp.float32),
        axis=2,
    )
    weight_of = jnp.where(filled, weights_flat[safe_source], jnp.zeros((), weights_flat.dtype))
    send_cot = (weight_of[:, None] * cotangent[token_of].astype(jnp.float32)).astype(jnp.bfloat16)
    cot_rows = deliver(send_cot.reshape(dp_count, capacity, width))
    d_hidden = jnp.einsum("rd,fd->rf", cot_rows, down_matrix, preferred_element_type=jnp.float32)
    d_gate = (d_hidden * up_pre * silu_slope).astype(jnp.bfloat16)
    d_up = (d_hidden * silu_value).astype(jnp.bfloat16)
    grad_down = jnp.einsum(
        "rf,rd->fd", hidden, cot_rows, preferred_element_type=jnp.float32
    ).astype(jnp.bfloat16)[None]
    grad_gate = jnp.einsum("rf,rd->fd", d_gate, x_rows, preferred_element_type=jnp.float32).astype(
        jnp.bfloat16
    )[None]
    grad_up = jnp.einsum("rf,rd->fd", d_up, x_rows, preferred_element_type=jnp.float32).astype(
        jnp.bfloat16
    )[None]
    shard_dx = jnp.dot(d_gate, gate_matrix, preferred_element_type=jnp.float32) + jnp.dot(
        d_up, up_matrix, preferred_element_type=jnp.float32
    )
    dx_back, dx_offset = send_back(shard_dx.astype(jnp.bfloat16), dp_count, capacity)
    route_dx = jnp.where(is_live[:, None] == 1, dx_back[safe_target], jnp.zeros((), dx_back.dtype))
    dx_part = jnp.sum(
        route_dx.astype(jnp.float32).reshape(tok_rows, top_count, piece_width), axis=1
    )
    mixed, grad_tokens, grad_route = (
        lax.psum_scatter(
            mixed_part.astype(jnp.bfloat16), "expert", scatter_dimension=0, tiled=True
        ).astype(jnp.float32),
        lax.psum_scatter(
            dx_part.astype(jnp.bfloat16), "expert", scatter_dimension=0, tiled=True
        ).astype(jnp.float32),
        lax.psum_scatter(
            route_grad.astype(jnp.bfloat16), "expert", scatter_dimension=0, tiled=True
        ).astype(jnp.float32),
    )
    return (
        mixed.astype(jnp.bfloat16),
        grad_tokens.astype(jnp.bfloat16),
        grad_route,
        grad_gate,
        grad_up,
        grad_down,
    )


FLOPS = 5_000_000_000
BYTES = 20_000_000


def dot_rows(left, right):
    return lax.dot_general(
        left, right, (((1,), (1,)), ((), ())), preferred_element_type=jnp.float32
    )


def dot_over_rows(left, right):
    return lax.dot_general(
        left, right, (((0,), (0,)), ((), ())), preferred_element_type=jnp.float32
    )


def padded(hidden_rows):
    return -(-hidden_rows // LANES) * LANES


def load_weights(refs, pre_buf, down_buf, sems):
    h = refs[0].shape[1]
    step = padded(h)
    copies = []
    for position, ref in enumerate(refs):
        buf, first = (pre_buf, position * step) if position < 4 else (down_buf, (position - 4) * step)
        copies.append(
            pltpu.make_async_copy(ref.at[0], buf.at[pl.ds(first, h)], sems.at[position])
        )
        if step > h:
            buf[first + h : first + step, :] = jnp.zeros((step - h, buf.shape[1]), buf.dtype)
    return copies


def dot_columns(out, left, right):
    for first in range(0, out.shape[1], COLUMN_TILE):
        there = pl.ds(first, min(COLUMN_TILE, out.shape[1] - first))
        out[:, there] = jnp.dot(
            left[...], right[:, there], preferred_element_type=jnp.float32
        ).astype(out.dtype)


def load_rows(refs, buf, sems):
    rows = buf.shape[0] // len(refs)
    return [
        pltpu.make_async_copy(
            ref.at[pl.ds(0, rows)], buf.at[pl.ds(position * rows, rows)], sems.at[position]
        )
        for position, ref in enumerate(refs)
    ]


def start(copies):
    for copy in copies:
        copy.start()


def wait(copies):
    for copy in copies:
        copy.wait()


def copies_between(pairs, sems):
    return [
        pltpu.make_async_copy(source, place, sems.at[position])
        for position, (source, place) in enumerate(pairs)
    ]


def forward_units(rows, weight, pre, hidden, weighted, to_gate, to_up):
    both = hidden.shape[1]
    for first in range(0, both, UNIT_TILE):
        there = pl.ds(first, UNIT_TILE)
        gate_pre = dot_rows(rows[...], pre[there])
        up_pre = dot_rows(rows[...], pre[pl.ds(both + first, UNIT_TILE)])
        silu_value, silu_slope = silu_parts(gate_pre)
        product = silu_value * up_pre
        hidden[:, there] = product.astype(jnp.bfloat16)
        weighted[:, there] = (product * weight[...]).astype(jnp.bfloat16)
        to_gate[:, there] = up_pre * silu_slope
        to_up[:, there] = silu_value


def backward_units(rows, weight, down, hidden, to_gate, to_up, d_pre, route_out):
    both = hidden.shape[1]
    route = None
    for first in range(0, both, UNIT_TILE):
        there = pl.ds(first, UNIT_TILE)
        plain = dot_rows(rows[...], down[there])
        term = jnp.sum(plain * hidden[:, there].astype(jnp.float32), axis=1, keepdims=True)
        route = term if route is None else route + term
        d_hidden = plain * weight[...]
        d_pre[:, there] = (d_hidden * to_gate[:, there]).astype(jnp.bfloat16)
        d_pre[:, pl.ds(both + first, UNIT_TILE)] = (d_hidden * to_up[:, there]).astype(jnp.bfloat16)
    route_out[...] = route


def both_halves(d_pre):
    both = d_pre.shape[1] // 2
    return d_pre.at[:, pl.ds(0, both)], d_pre.at[:, pl.ds(both, both)]


def forward_kernel(
    gate, gate_other, up, up_other, down, down_other, x_first, x_second, weight,
    mixed_out, hidden_out, weighted_out, to_gate_out, to_up_out,
    pre_buf, down_buf, row_buf, mixed, hidden, weighted, to_gate, to_up,
    sems, row_sems, out_sems,
):
    loads = load_weights(
        (gate, gate_other, up, up_other, down, down_other), pre_buf, down_buf, sems
    )
    rows = load_rows((x_first, x_second), row_buf, row_sems)
    kept = (hidden, weighted, to_gate, to_up)
    outs = (hidden_out, weighted_out, to_gate_out, to_up_out)
    stores = copies_between(((mixed, mixed_out), *zip(kept, outs)), out_sems)
    start(rows + loads)
    wait(rows + loads[:4])
    forward_units(row_buf, weight, pre_buf, *kept)
    start(stores[1:])
    wait(loads[4:])
    dot_columns(mixed, weighted, down_buf)
    start(stores[:1])
    wait(stores)


def backward_kernel(
    gate, gate_other, up, up_other, down, down_other, cot_first, cot_second, weight,
    hidden_in, to_gate_in, to_up_in,
    dx_out, route_out, d_gate_out, d_up_out,
    pre_buf, down_buf, row_buf, dx, d_pre, hidden, to_gate, to_up,
    sems, row_sems, in_sems, out_sems,
):
    loads = load_weights(
        (gate, gate_other, up, up_other, down, down_other), pre_buf, down_buf, sems
    )
    rows = load_rows((cot_first, cot_second), row_buf, row_sems)
    kept = (hidden, to_gate, to_up)
    parts = copies_between(zip((hidden_in, to_gate_in, to_up_in), kept), in_sems)
    d_gate, d_up = both_halves(d_pre)
    stores = copies_between(((dx, dx_out), (d_gate, d_gate_out), (d_up, d_up_out)), out_sems)
    start(rows + loads[4:] + parts + loads[:4])
    wait(rows + loads[4:] + parts)
    backward_units(row_buf, weight, down_buf, *kept, d_pre, route_out)
    start(stores[1:])
    wait(loads[:4])
    dot_columns(dx, d_pre, pre_buf)
    start(stores[:1])
    wait(stores)


def middle_kernel(
    gate, gate_other, up, up_other, down, down_other,
    x_first, x_second, cot_first, cot_second, weight34, weight12,
    hidden_in, to_gate_in, to_up_in,
    mixed_out, hidden_out, weighted_out, to_gate_out, to_up_out,
    dx_out, route_out, d_gate_out, d_up_out,
    pre_buf, down_buf, row_buf, cot_buf,
    mixed, hidden34, weighted34, to_gate34, to_up34, dx, d_pre, hidden12, to_gate12, to_up12,
    sems, row_sems, cot_sems, in_sems, out_sems, back_sems,
):
    loads = load_weights(
        (gate, gate_other, up, up_other, down, down_other), pre_buf, down_buf, sems
    )
    rows = load_rows((x_first, x_second), row_buf, row_sems)
    cots = load_rows((cot_first, cot_second), cot_buf, cot_sems)
    kept34 = (hidden34, weighted34, to_gate34, to_up34)
    kept12 = (hidden12, to_gate12, to_up12)
    parts = copies_between(zip((hidden_in, to_gate_in, to_up_in), kept12), in_sems)
    outs = (hidden_out, weighted_out, to_gate_out, to_up_out)
    stores = copies_between(((mixed, mixed_out), *zip(kept34, outs)), out_sems)
    d_gate, d_up = both_halves(d_pre)
    back = copies_between(((dx, dx_out), (d_gate, d_gate_out), (d_up, d_up_out)), back_sems)
    start(rows + loads + cots + parts)
    wait(rows + loads[:4])
    forward_units(row_buf, weight34, pre_buf, *kept34)
    start(stores[1:])
    wait(loads[4:])
    dot_columns(mixed, weighted34, down_buf)
    start(stores[:1])
    wait(cots + parts)
    backward_units(cot_buf, weight12, down_buf, *kept12, d_pre, route_out)
    start(back[1:])
    dot_columns(dx, d_pre, pre_buf)
    start(back[:1])
    wait(stores + back)


WIDE, NARROW = 8, 6


def weight_products(refs, first, count):
    xs, gs, narrow = refs[:4], refs[4:WIDE], refs[WIDE : WIDE + NARROW]
    rows = narrow[0].shape[0] // 2
    there = pl.ds(first, count)

    def product(pair, parts):
        total = None
        for position, part in enumerate(parts):
            here = pl.ds(position % 2 * rows, rows)
            term = dot_over_rows(pair[position // 2][here, there], part[...])
            total = term if total is None else total + term
        return total

    return product(narrow[0:2], xs), product(narrow[2:4], xs), product(narrow[4:6], gs)


def other_grads_kernel(*refs):
    out = refs[-1]
    count = refs[WIDE].shape[1] // 2
    h = out.shape[1]
    for position, product in enumerate(weight_products(refs, count, count)):
        out[position] = product[:h].astype(jnp.bfloat16)


def own_grads_kernel(*refs):
    received, outs = refs[WIDE + NARROW], refs[WIDE + NARROW + 1 :]
    count = refs[WIDE].shape[1] // 2
    h = received.shape[1]
    for position, product in enumerate(weight_products(refs, 0, count)):
        total = product[:h] + received[position].astype(jnp.float32)
        outs[position][0] = total.astype(jnp.bfloat16)


def cost():
    return pl.CostEstimate(flops=FLOPS, bytes_accessed=BYTES, transcendentals=0)


def specs(space, count):
    return [pl.BlockSpec(memory_space=space)] * count


def buffers_for(arrays):
    return [pltpu.VMEM(array.shape, array.dtype) for array in arrays]


def row_kernel(kernel, name, matrices, pairs, weights, parts, outs, in_vmem, buffers, counts):
    _, h, width = matrices[0].shape
    step = padded(h)
    rows = weights[0].shape[0]
    space = [pltpu.VMEM if position in in_vmem else pl.ANY for position in range(len(outs))]
    own = [jax.ShapeDtypeStruct((n, width), jnp.bfloat16) for n in (4 * step, 2 * step)]
    own += [jax.ShapeDtypeStruct((rows, width), jnp.bfloat16)] * (len(pairs) // 2)
    return pl.pallas_call(
        kernel,
        out_shape=outs,
        in_specs=specs(pl.ANY, len(matrices) + len(pairs))
        + specs(pltpu.VMEM, len(weights))
        + specs(pl.ANY, len(parts)),
        out_specs=[pl.BlockSpec(memory_space=kind) for kind in space],
        scratch_shapes=buffers_for((*own, *buffers, *parts))
        + [pltpu.SemaphoreType.DMA((count,)) for count in counts],
        compiler_params=pltpu.CompilerParams(vmem_limit_bytes=VMEM_LIMIT),
        cost_estimate=cost(),
        name=name,
    )(*matrices, *pairs, *weights, *parts)


def forward_outs(matrices, weight):
    rows, width = weight.shape[0], matrices[0].shape[2]
    units = 2 * padded(matrices[0].shape[1])
    f32, bf16 = jnp.float32, jnp.bfloat16
    outs = [jax.ShapeDtypeStruct((rows, width), bf16)]
    return outs + [jax.ShapeDtypeStruct((rows, units), kind) for kind in (bf16, bf16, f32, f32)]


def backward_outs(matrices, weight):
    rows, width = weight.shape[0], matrices[0].shape[2]
    units = 2 * padded(matrices[0].shape[1])
    f32, bf16 = jnp.float32, jnp.bfloat16
    outs = [jax.ShapeDtypeStruct((rows, width), bf16), jax.ShapeDtypeStruct((rows, 1), f32)]
    outs += [jax.ShapeDtypeStruct((rows, units), bf16)] * 2
    return outs, [outs[0], jax.ShapeDtypeStruct((rows, 2 * units), bf16)]


def forward(matrices, pair, weight):
    outs = forward_outs(matrices, weight)
    return row_kernel(
        forward_kernel, "forward", matrices, pair, (weight,), (), outs, (), outs, (6, 2, 5)
    )


def backward(matrices, pair, weight, parts):
    outs, buffers = backward_outs(matrices, weight)
    return row_kernel(
        backward_kernel, "backward", matrices, pair, (weight,), parts, outs, (1,), buffers,
        (6, 2, 3, 3),
    )


def middle(matrices, pair34, pair12, weight34, weight12, parts12):
    ahead = forward_outs(matrices, weight34)
    back, buffers = backward_outs(matrices, weight12)
    result = row_kernel(
        middle_kernel, "middle", matrices, (*pair34, *pair12), (weight34, weight12), parts12,
        ahead + back, (len(ahead) + 1,), ahead + buffers, (6, 2, 2, 3, 5, 3),
    )
    return result[: len(ahead)], result[len(ahead) :]


def weight_grads(wide, narrow, h, received=None):
    rows, width = narrow[0].shape[0] // 2, wide[0].shape[1]
    tile = min(512, width)
    tall = pl.BlockSpec((rows, tile), lambda n: (0, n))
    whole = pl.BlockSpec(narrow[0].shape, lambda n: (0, 0), pipeline_mode=pl.Buffered(1))
    three = pl.BlockSpec((3, h, tile), lambda n: (0, 0, n))
    in_specs = [tall] * len(wide) + [whole] * len(narrow)
    if received is None:
        kernel, more, name = other_grads_kernel, (), "other_grads"
        outs = jax.ShapeDtypeStruct((3, h, width), jnp.bfloat16)
        out_specs = three
    else:
        kernel, more, name = own_grads_kernel, (received,), "own_grads"
        outs = [jax.ShapeDtypeStruct((1, h, width), jnp.bfloat16)] * 3
        out_specs = [pl.BlockSpec((1, h, tile), lambda n: (0, 0, n))] * 3
        in_specs = in_specs + [three]
    return pl.pallas_call(
        kernel,
        out_shape=outs,
        grid=(width // tile,),
        in_specs=in_specs,
        out_specs=out_specs,
        compiler_params=pltpu.CompilerParams(vmem_limit_bytes=VMEM_LIMIT),
        cost_estimate=cost(),
        name=name,
    )(*wide, *narrow, *more)


def all_slots_body(tokens, routes, route_weight, w_gate, w_up, w_down, grad_out):
    f32 = jnp.float32
    dp_count = lax.axis_size("dp")
    ex_count = lax.axis_size("expert")
    levels = ex_count // CORES
    groups = ex_count // SHARDS
    width = tokens.shape[1]
    block = grad_out.shape[0]
    half = levels * block
    dp_index = lax.axis_index("dp")
    ex_index = lax.axis_index("expert")
    level, core = ex_index // CORES, ex_index % CORES

    def pieces(values):
        rest, parts = values.reshape(-1), []
        for _ in range(3):
            part = lax.reduce_precision(rest, 8, 7)
            parts.append(part.astype(jnp.bfloat16))
            rest = rest - part
        row = jnp.concatenate(parts)
        row = jnp.pad(row, (0, PACKED_ROWS * width - row.shape[0]))
        return row.reshape(PACKED_ROWS, width)

    def whole(message, position):
        row = message[half : half + PACKED_ROWS].reshape(-1)[: 9 * half]
        parts = row.reshape(3, 3, half)[:, position].astype(f32)
        return (parts[0] + parts[1]) + parts[2]

    def exchange(value, partner):
        pairs = []
        for d in range(dp_count):
            for e in range(ex_count):
                other_d, other_e = partner(d, e // CORES, e % CORES)
                pairs.append((d * ex_count + e, other_d * ex_count + other_e))
        return lax.ppermute(value, ("dp", "expert"), pairs)

    def to_near(value):
        return exchange(value, lambda d, z, c: (d ^ (1 + c), z * CORES + c))

    def to_far(value):
        return exchange(value, lambda d, z, c: (d ^ (2 - c), z * CORES + c))

    def to_core(value):
        return exchange(value, lambda d, z, c: (d, z * CORES + 1 - c))

    def to_level(value, step):
        return exchange(value, lambda d, z, c: (d, (z ^ step) * CORES + c))

    def add(*terms):
        total = terms[0].astype(f32)
        for term in terms[1:]:
            total = total + term.astype(f32)
        return total.astype(terms[0].dtype)

    def after(value, *others):
        return lax.optimization_barrier((value, *others))[0]

    def in_blocks(terms):
        return [term.reshape(levels, block, term.shape[-1]) for term in terms]

    def by_blocks(terms, *wait_for):
        terms = in_blocks(terms)
        received = [
            to_level(add(*[term[k] for term in terms]), step)
            for k, step in enumerate(LEVEL_STEPS)
            if k > 0
        ]
        own = after(terms[0][0], *wait_for)
        return add(own, *[term[0] for term in terms[1:]], *received)

    level_order = jnp.array(LEVEL_STEPS, jnp.int32) ^ level
    block_order = level_order * CORES + core
    near, far = dp_index ^ (1 + core), dp_index ^ (2 - core)
    group_dp = (dp_index, near, far, dp_index ^ 3)

    group_experts = jnp.arange(dp_count, dtype=jnp.int32) * groups + ex_index // SHARDS
    table = jnp.sum(
        jnp.where(routes[None] == group_experts[:, None, None], route_weight[None], 0.0), axis=2
    )
    table = table.reshape(dp_count, ex_count, block)[:, block_order]
    own_table, near_table, far_table, diagonal_table = (
        lax.dynamic_index_in_dim(table, d, axis=0).reshape(half) for d in group_dp
    )

    x_own = tokens.reshape(ex_count, block, width)[block_order].reshape(half, width)
    x_own = jnp.concatenate(
        [x_own, pieces(jnp.stack([near_table, far_table, diagonal_table]))], axis=0
    )
    x_near = to_near(x_own)
    x_far = to_far(x_own)
    others = [to_core(matrix) for matrix in (w_gate, w_up, w_down)]
    matrices = (w_gate, others[0], w_up, others[1], w_down, others[2])
    cotangent = after(grad_out, x_own)
    g_pair = jnp.concatenate([cotangent, to_level(cotangent, 2)], axis=0)
    x_last = to_far(after(x_near, x_far))
    weight12 = jnp.concatenate([own_table, whole(x_near, 0)])[:, None]
    weight34 = jnp.concatenate([whole(x_far, 1), whole(x_last, 2)])[:, None]

    mixed12, hidden12, weighted12, *slopes12 = forward(matrices, (x_own, x_near), weight12)
    x_last = after(x_last, mixed12)
    g_own = jnp.concatenate([g_pair, to_level(g_pair, 1)], axis=0)
    g_own = after(g_own, x_near, x_far)
    g_near = to_near(g_own)
    g_far = to_far(after(g_own, x_last, g_near))
    g_last = to_far(after(g_near, x_last))
    ahead, back = middle(
        matrices, (x_far, x_last), (g_own, g_near), weight34, weight12, (hidden12, *slopes12)
    )
    mixed34, hidden34, weighted34, *slopes34 = ahead
    dx12, route12, gate12, up12 = back
    g_last = after(g_last, mixed34)
    dx34, route34, gate34, up34 = backward(
        matrices, (g_far, g_last), weight34, (hidden34, *slopes34)
    )

    mixed_far = to_far(after(mixed34, g_far, g_last))
    mixed_part = add(mixed12[half:], after(mixed_far, dx34)[half:])
    mixed_near = to_near(mixed_part)

    mixed_terms = in_blocks((mixed12[:half], mixed_far[:half], mixed_near))
    mixed_pair = add(*[term[2:] for term in mixed_terms])
    dx_far = to_far(dx34)
    dx_part = add(dx12[half:], after(dx_far, mixed_pair)[half:])
    dx_near = to_near(dx_part)
    mixed_pair = after(to_level(mixed_pair, 1), dx_part)
    mixed_last = to_level(add(*[term[1] for term in mixed_terms], mixed_pair[1]), 2)

    h = w_gate.shape[1]
    wide = (x_own, x_near, x_far, x_last, g_own, g_near, g_far, g_last)
    narrow = after((gate12, gate34, up12, up34, weighted12, weighted34), mixed_far)
    received = to_core(weight_grads(wide, narrow, h))
    grads = weight_grads(wide, narrow, h, received)

    route = jnp.concatenate([route12, route34]).reshape(dp_count, levels, block)
    pair = after(to_level(route[:, 2:], 1), mixed_part)
    other_group = after(to_level(route[:, 1] + pair[:, 1], 2), mixed_near)
    route = jnp.stack([route[:, 0] + pair[:, 0], other_group], axis=1)
    route_far = after(to_far(route[2:]), dx_near)
    route_near = to_near(jnp.stack([route[1], route_far[1]]))

    mixed_last = after(mixed_last, *grads)
    mixed = add(*[term[0] for term in mixed_terms], mixed_pair[0], mixed_last)
    grad_tokens = by_blocks((dx12[:half], dx_far[:half], dx_near), *grads)

    route_own = jnp.stack([route[0], route_far[0], route_near[0], route_near[1]])
    my_routes = lax.dynamic_slice_in_dim(routes, ex_index * block, block, axis=0)
    my_group = ex_index // SHARDS
    grad_route = jnp.zeros(my_routes.shape, f32)
    for which, group in enumerate((my_group, 1 - my_group)):
        for position, d in enumerate((dp_index, far, near, dp_index ^ 3)):
            grad_route = grad_route + jnp.where(
                my_routes == d * groups + group, route_own[position, which][:, None], 0.0
            )
    return (mixed, grad_tokens, grad_route, *grads)


def body(tokens, routes, *rest):
    dp_count = lax.axis_size("dp")
    ex_count = lax.axis_size("expert")
    tok_rows, top_count = routes.shape
    expert_count = dp_count * ex_count // SHARDS
    every_slot = 3 * tok_rows * top_count >= 2 * expert_count * tok_rows
    if every_slot and dp_count == 4 and ex_count == CORES * len(LEVEL_STEPS):
        return all_slots_body(tokens, routes, *rest)
    return padded_body(tokens, routes, *rest)


def solution(mesh):
    return jax.shard_map(
        body,
        mesh=mesh,
        in_specs=(
            P("dp", None),
            P("dp", None),
            P("dp", None),
            P(("dp", "expert"), None, None),
            P(("dp", "expert"), None, None),
            P(("dp", "expert"), None, None),
            P(("dp", "expert"), None),
        ),
        out_specs=(
            P(("dp", "expert"), None),
            P(("dp", "expert"), None),
            P(("dp", "expert"), None),
            P(("dp", "expert"), None, None),
            P(("dp", "expert"), None, None),
            P(("dp", "expert"), None, None),
        ),
        check_vma=False,
    )
```

```python
import jax
import jax.numpy as jnp
from jax import lax
from jax.experimental import pallas as pl
from jax.experimental.pallas import tpu as pltpu
from jax.sharding import PartitionSpec as P

SHARDS = 4
CORES = 2
LANES = 128
UNIT_TILE = 256
COLUMN_TILE = 512
LEVEL_STEPS = (0, 2, 1, 3)
PACKED_ROWS = 16
VMEM_LIMIT = 56 * 1024 * 1024


def silu_parts(gate_pre):
    sigma = jax.nn.sigmoid(gate_pre)
    return (gate_pre * sigma, sigma * (1.0 + gate_pre * (1.0 - sigma)))


def deliver(buffer):
    dp_count, slot_count, width = buffer.shape
    arrived = lax.all_to_all(buffer, "dp", split_axis=0, concat_axis=0, tiled=True)
    return arrived.reshape(dp_count * slot_count, width)


def send_back(rows, dp_count, slot_count):
    width = rows.shape[1]
    returned = lax.all_to_all(
        rows.reshape(dp_count, slot_count, width), "dp", split_axis=0, concat_axis=0, tiled=True
    )
    return (returned.reshape(dp_count * slot_count, width), jnp.zeros((), jnp.int32))


def padded_body(tokens, routes, route_weight, w_gate, w_up, w_down, grad_out):
    dp_count = lax.axis_size("dp")
    ex_count = lax.axis_size("expert")
    groups = ex_count // SHARDS
    my_group = lax.axis_index("expert") // SHARDS
    tok_rows, top_count = routes.shape
    width = tokens.shape[1]
    expert_count = dp_count * groups
    capacity = min(tok_rows, 3 * tok_rows * top_count // (2 * expert_count))
    flat_routes = routes.reshape(-1)
    route_count = flat_routes.shape[0]
    owner_ids = jnp.arange(dp_count, dtype=jnp.int32) * groups + my_group
    hit_table = (flat_routes[:, None] == owner_ids[None, :]).astype(jnp.int32)
    is_live = jnp.sum(hit_table, axis=1)
    owner_dp = jnp.sum(hit_table * jnp.arange(dp_count, dtype=jnp.int32)[None, :], axis=1)
    slot_index = jnp.sum((jnp.cumsum(hit_table, axis=0) - 1) * hit_table, axis=1)
    dump_row = dp_count * capacity
    target = jnp.where(is_live == 1, owner_dp * capacity + slot_index, dump_row)
    source = (
        jnp.full((dump_row + 1,), route_count, jnp.int32)
        .at[target]
        .set(jnp.arange(route_count, dtype=jnp.int32))[:dump_row]
    )
    filled = source < route_count
    safe_source = jnp.where(filled, source, 0)
    token_of = safe_source // top_count
    weights_flat = route_weight.reshape(-1)
    send_rows = jnp.where(filled[:, None], tokens[token_of], jnp.zeros((), tokens.dtype))
    x_rows = deliver(send_rows.reshape(dp_count, capacity, width))
    gate_matrix = w_gate[0]
    up_matrix = w_up[0]
    down_matrix = w_down[0]
    gate_pre = jnp.einsum("rd,fd->rf", x_rows, gate_matrix, preferred_element_type=jnp.float32)
    up_pre = jnp.einsum("rd,fd->rf", x_rows, up_matrix, preferred_element_type=jnp.float32)
    silu_value, silu_slope = silu_parts(gate_pre)
    hidden = (silu_value * up_pre).astype(jnp.bfloat16)
    shard_part = jnp.dot(hidden, down_matrix, preferred_element_type=jnp.float32).astype(
        jnp.bfloat16
    )
    returned, offset = send_back(shard_part, dp_count, capacity)
    piece_width = returned.shape[1]
    safe_target = jnp.where(is_live == 1, target, 0)
    route_part = jnp.where(
        is_live[:, None] == 1, returned[safe_target], jnp.zeros((), returned.dtype)
    )
    weighted = weights_flat[:, None] * route_part.astype(jnp.float32)
    mixed_part = jnp.sum(weighted.reshape(tok_rows, top_count, piece_width), axis=1)
    cotangent = lax.all_gather(grad_out, "expert", axis=0, tiled=True)
    route_grad = jnp.sum(
        route_part.reshape(tok_rows, top_count, piece_width).astype(jnp.float32)
        * cotangent[:, None, :].astype(jnp.float32),
        axis=2,
    )
    weight_of = jnp.where(filled, weights_flat[safe_source], jnp.zeros((), weights_flat.dtype))
    send_cot = (weight_of[:, None] * cotangent[token_of].astype(jnp.float32)).astype(jnp.bfloat16)
    cot_rows = deliver(send_cot.reshape(dp_count, capacity, width))
    d_hidden = jnp.einsum("rd,fd->rf", cot_rows, down_matrix, preferred_element_type=jnp.float32)
    d_gate = (d_hidden * up_pre * silu_slope).astype(jnp.bfloat16)
    d_up = (d_hidden * silu_value).astype(jnp.bfloat16)
    grad_down = jnp.einsum(
        "rf,rd->fd", hidden, cot_rows, preferred_element_type=jnp.float32
    ).astype(jnp.bfloat16)[None]
    grad_gate = jnp.einsum("rf,rd->fd", d_gate, x_rows, preferred_element_type=jnp.float32).astype(
        jnp.bfloat16
    )[None]
    grad_up = jnp.einsum("rf,rd->fd", d_up, x_rows, preferred_element_type=jnp.float32).astype(
        jnp.bfloat16
    )[None]
    shard_dx = jnp.dot(d_gate, gate_matrix, preferred_element_type=jnp.float32) + jnp.dot(
        d_up, up_matrix, preferred_element_type=jnp.float32
    )
    dx_back, dx_offset = send_back(shard_dx.astype(jnp.bfloat16), dp_count, capacity)
    route_dx = jnp.where(is_live[:, None] == 1, dx_back[safe_target], jnp.zeros((), dx_back.dtype))
    dx_part = jnp.sum(
        route_dx.astype(jnp.float32).reshape(tok_rows, top_count, piece_width), axis=1
    )
    mixed, grad_tokens, grad_route = (
        lax.psum_scatter(
            mixed_part.astype(jnp.bfloat16), "expert", scatter_dimension=0, tiled=True
        ).astype(jnp.float32),
        lax.psum_scatter(
            dx_part.astype(jnp.bfloat16), "expert", scatter_dimension=0, tiled=True
        ).astype(jnp.float32),
        lax.psum_scatter(
            route_grad.astype(jnp.bfloat16), "expert", scatter_dimension=0, tiled=True
        ).astype(jnp.float32),
    )
    return (
        mixed.astype(jnp.bfloat16),
        grad_tokens.astype(jnp.bfloat16),
        grad_route,
        grad_gate,
        grad_up,
        grad_down,
    )


FLOPS = 5_000_000_000
BYTES = 20_000_000


def dot_rows(left, right):
    return lax.dot_general(
        left, right, (((1,), (1,)), ((), ())), preferred_element_type=jnp.float32
    )


def dot_over_rows(left, right):
    return lax.dot_general(
        left, right, (((0,), (0,)), ((), ())), preferred_element_type=jnp.float32
    )


def padded(hidden_rows):
    return -(-hidden_rows // LANES) * LANES


def load_weights(refs, pre_buf, down_buf, sems):
    h = refs[0].shape[1]
    step = padded(h)
    copies = []
    for position, ref in enumerate(refs):
        buf, first = (pre_buf, position * step) if position < 4 else (down_buf, (position - 4) * step)
        copies.append(
            pltpu.make_async_copy(ref.at[0], buf.at[pl.ds(first, h)], sems.at[position])
        )
        if step > h:
            buf[first + h : first + step, :] = jnp.zeros((step - h, buf.shape[1]), buf.dtype)
    return copies


def dot_columns(out, left, right):
    for first in range(0, out.shape[1], COLUMN_TILE):
        there = pl.ds(first, min(COLUMN_TILE, out.shape[1] - first))
        out[:, there] = jnp.dot(
            left[...], right[:, there], preferred_element_type=jnp.float32
        ).astype(out.dtype)


def load_rows(refs, buf, sems):
    rows = buf.shape[0] // len(refs)
    return [
        pltpu.make_async_copy(
            ref.at[pl.ds(0, rows)], buf.at[pl.ds(position * rows, rows)], sems.at[position]
        )
        for position, ref in enumerate(refs)
    ]


def start(copies):
    for copy in copies:
        copy.start()


def wait(copies):
    for copy in copies:
        copy.wait()


def copies_between(pairs, sems):
    return [
        pltpu.make_async_copy(source, place, sems.at[position])
        for position, (source, place) in enumerate(pairs)
    ]


def forward_units(rows, weight, pre, hidden, weighted, to_gate, to_up):
    both = hidden.shape[1]
    for first in range(0, both, UNIT_TILE):
        there = pl.ds(first, UNIT_TILE)
        gate_pre = dot_rows(rows[...], pre[there])
        up_pre = dot_rows(rows[...], pre[pl.ds(both + first, UNIT_TILE)])
        silu_value, silu_slope = silu_parts(gate_pre)
        product = silu_value * up_pre
        hidden[:, there] = product.astype(jnp.bfloat16)
        weighted[:, there] = (product * weight[...]).astype(jnp.bfloat16)
        to_gate[:, there] = up_pre * silu_slope
        to_up[:, there] = silu_value


def backward_units(rows, weight, down, parts, hidden, to_gate, to_up, d_pre, route_out):
    both = hidden.shape[1]
    route = None
    for first in range(0, both, UNIT_TILE):
        there = pl.ds(first, UNIT_TILE)
        plain = dot_rows(rows[...], down[there])
        if first == 0:
            wait(parts)
        term = jnp.sum(plain * hidden[:, there].astype(jnp.float32), axis=1, keepdims=True)
        route = term if route is None else route + term
        d_hidden = plain * weight[...]
        d_pre[:, there] = (d_hidden * to_gate[:, there]).astype(jnp.bfloat16)
        d_pre[:, pl.ds(both + first, UNIT_TILE)] = (d_hidden * to_up[:, there]).astype(jnp.bfloat16)
    route_out[...] = route


def both_halves(d_pre):
    both = d_pre.shape[1] // 2
    return d_pre.at[:, pl.ds(0, both)], d_pre.at[:, pl.ds(both, both)]


def forward_kernel(
    gate, gate_other, up, up_other, down, down_other, x_first, x_second, weight,
    mixed_out, hidden_out, weighted_out, to_gate_out, to_up_out,
    pre_buf, down_buf, row_buf, mixed, hidden, weighted, to_gate, to_up,
    sems, row_sems, out_sems,
):
    loads = load_weights(
        (gate, gate_other, up, up_other, down, down_other), pre_buf, down_buf, sems
    )
    rows = load_rows((x_first, x_second), row_buf, row_sems)
    kept = (hidden, weighted, to_gate, to_up)
    outs = (hidden_out, weighted_out, to_gate_out, to_up_out)
    stores = copies_between(((mixed, mixed_out), *zip(kept, outs)), out_sems)
    start(rows + loads)
    wait(rows + loads[:4])
    forward_units(row_buf, weight, pre_buf, *kept)
    start(stores[1:])
    wait(loads[4:])
    dot_columns(mixed, weighted, down_buf)
    start(stores[:1])
    wait(stores)


def backward_kernel(
    gate, gate_other, up, up_other, down, down_other, cot_first, cot_second, weight,
    hidden_in, to_gate_in, to_up_in,
    dx_out, route_out, d_gate_out, d_up_out,
    pre_buf, down_buf, row_buf, dx, d_pre, hidden, to_gate, to_up,
    sems, row_sems, in_sems, out_sems,
):
    loads = load_weights(
        (gate, gate_other, up, up_other, down, down_other), pre_buf, down_buf, sems
    )
    rows = load_rows((cot_first, cot_second), row_buf, row_sems)
    kept = (hidden, to_gate, to_up)
    parts = copies_between(zip((hidden_in, to_gate_in, to_up_in), kept), in_sems)
    d_gate, d_up = both_halves(d_pre)
    stores = copies_between(((dx, dx_out), (d_gate, d_gate_out), (d_up, d_up_out)), out_sems)
    start(rows + loads[4:] + parts + loads[:4])
    wait(rows + loads[4:])
    backward_units(row_buf, weight, down_buf, parts, *kept, d_pre, route_out)
    start(stores[1:])
    wait(loads[:4])
    dot_columns(dx, d_pre, pre_buf)
    start(stores[:1])
    wait(stores)


def middle_kernel(
    gate, gate_other, up, up_other, down, down_other,
    x_first, x_second, cot_first, cot_second, weight34, weight12,
    hidden_in, to_gate_in, to_up_in,
    mixed_out, hidden_out, weighted_out, to_gate_out, to_up_out,
    dx_out, route_out, d_gate_out, d_up_out,
    pre_buf, down_buf, row_buf, cot_buf,
    mixed, hidden34, weighted34, to_gate34, to_up34, dx, d_pre, hidden12, to_gate12, to_up12,
    sems, row_sems, cot_sems, in_sems, out_sems, back_sems,
):
    loads = load_weights(
        (gate, gate_other, up, up_other, down, down_other), pre_buf, down_buf, sems
    )
    rows = load_rows((x_first, x_second), row_buf, row_sems)
    cots = load_rows((cot_first, cot_second), cot_buf, cot_sems)
    kept34 = (hidden34, weighted34, to_gate34, to_up34)
    kept12 = (hidden12, to_gate12, to_up12)
    parts = copies_between(zip((hidden_in, to_gate_in, to_up_in), kept12), in_sems)
    outs = (hidden_out, weighted_out, to_gate_out, to_up_out)
    stores = copies_between(((mixed, mixed_out), *zip(kept34, outs)), out_sems)
    d_gate, d_up = both_halves(d_pre)
    back = copies_between(((dx, dx_out), (d_gate, d_gate_out), (d_up, d_up_out)), back_sems)
    start(rows + loads + cots + parts)
    wait(rows + loads[:4])
    forward_units(row_buf, weight34, pre_buf, *kept34)
    start(stores[1:])
    wait(loads[4:])
    dot_columns(mixed, weighted34, down_buf)
    start(stores[:1])
    wait(cots)
    backward_units(cot_buf, weight12, down_buf, parts, *kept12, d_pre, route_out)
    start(back[1:])
    dot_columns(dx, d_pre, pre_buf)
    start(back[:1])
    wait(stores + back)


WIDE, NARROW = 8, 6


def weight_products(refs, first, count):
    xs, gs, narrow = refs[:4], refs[4:WIDE], refs[WIDE : WIDE + NARROW]
    rows = narrow[0].shape[0] // 2
    there = pl.ds(first, count)

    def product(pair, parts):
        total = None
        for position, part in enumerate(parts):
            here = pl.ds(position % 2 * rows, rows)
            term = dot_over_rows(pair[position // 2][here, there], part[...])
            total = term if total is None else total + term
        return total

    return product(narrow[0:2], xs), product(narrow[2:4], xs), product(narrow[4:6], gs)


def other_grads_kernel(*refs):
    out = refs[-1]
    count = refs[WIDE].shape[1] // 2
    h = out.shape[1]
    for position, product in enumerate(weight_products(refs, count, count)):
        out[position] = product[:h].astype(jnp.bfloat16)


def own_grads_kernel(*refs):
    received, outs = refs[WIDE + NARROW], refs[WIDE + NARROW + 1 :]
    count = refs[WIDE].shape[1] // 2
    h = received.shape[1]
    for position, product in enumerate(weight_products(refs, 0, count)):
        total = product[:h] + received[position].astype(jnp.float32)
        outs[position][0] = total.astype(jnp.bfloat16)


def cost():
    return pl.CostEstimate(flops=FLOPS, bytes_accessed=BYTES, transcendentals=0)


def specs(space, count):
    return [pl.BlockSpec(memory_space=space)] * count


def buffers_for(arrays):
    return [pltpu.VMEM(array.shape, array.dtype) for array in arrays]


def row_kernel(kernel, name, matrices, pairs, weights, parts, outs, in_vmem, buffers, counts):
    _, h, width = matrices[0].shape
    step = padded(h)
    rows = weights[0].shape[0]
    space = [pltpu.VMEM if position in in_vmem else pl.ANY for position in range(len(outs))]
    own = [jax.ShapeDtypeStruct((n, width), jnp.bfloat16) for n in (4 * step, 2 * step)]
    own += [jax.ShapeDtypeStruct((rows, width), jnp.bfloat16)] * (len(pairs) // 2)
    return pl.pallas_call(
        kernel,
        out_shape=outs,
        in_specs=specs(pl.ANY, len(matrices) + len(pairs))
        + specs(pltpu.VMEM, len(weights))
        + specs(pl.ANY, len(parts)),
        out_specs=[pl.BlockSpec(memory_space=kind) for kind in space],
        scratch_shapes=buffers_for((*own, *buffers, *parts))
        + [pltpu.SemaphoreType.DMA((count,)) for count in counts],
        compiler_params=pltpu.CompilerParams(vmem_limit_bytes=VMEM_LIMIT),
        cost_estimate=cost(),
        name=name,
    )(*matrices, *pairs, *weights, *parts)


def forward_outs(matrices, weight):
    rows, width = weight.shape[0], matrices[0].shape[2]
    units = 2 * padded(matrices[0].shape[1])
    f32, bf16 = jnp.float32, jnp.bfloat16
    outs = [jax.ShapeDtypeStruct((rows, width), bf16)]
    return outs + [jax.ShapeDtypeStruct((rows, units), kind) for kind in (bf16, bf16, f32, f32)]


def backward_outs(matrices, weight):
    rows, width = weight.shape[0], matrices[0].shape[2]
    units = 2 * padded(matrices[0].shape[1])
    f32, bf16 = jnp.float32, jnp.bfloat16
    outs = [jax.ShapeDtypeStruct((rows, width), bf16), jax.ShapeDtypeStruct((rows, 1), f32)]
    outs += [jax.ShapeDtypeStruct((rows, units), bf16)] * 2
    return outs, [outs[0], jax.ShapeDtypeStruct((rows, 2 * units), bf16)]


def forward(matrices, pair, weight):
    outs = forward_outs(matrices, weight)
    return row_kernel(
        forward_kernel, "forward", matrices, pair, (weight,), (), outs, (), outs, (6, 2, 5)
    )


def backward(matrices, pair, weight, parts):
    outs, buffers = backward_outs(matrices, weight)
    return row_kernel(
        backward_kernel, "backward", matrices, pair, (weight,), parts, outs, (1,), buffers,
        (6, 2, 3, 3),
    )


def middle(matrices, pair34, pair12, weight34, weight12, parts12):
    ahead = forward_outs(matrices, weight34)
    back, buffers = backward_outs(matrices, weight12)
    result = row_kernel(
        middle_kernel, "middle", matrices, (*pair34, *pair12), (weight34, weight12), parts12,
        ahead + back, (len(ahead) + 1,), ahead + buffers, (6, 2, 2, 3, 5, 3),
    )
    return result[: len(ahead)], result[len(ahead) :]


def weight_grads(wide, narrow, h, received=None):
    rows, width = narrow[0].shape[0] // 2, wide[0].shape[1]
    tile = min(512, width)
    tall = pl.BlockSpec((rows, tile), lambda n: (0, n))
    whole = pl.BlockSpec(narrow[0].shape, lambda n: (0, 0), pipeline_mode=pl.Buffered(1))
    three = pl.BlockSpec((3, h, tile), lambda n: (0, 0, n))
    in_specs = [tall] * len(wide) + [whole] * len(narrow)
    if received is None:
        kernel, more, name = other_grads_kernel, (), "other_grads"
        outs = jax.ShapeDtypeStruct((3, h, width), jnp.bfloat16)
        out_specs = three
    else:
        kernel, more, name = own_grads_kernel, (received,), "own_grads"
        outs = [jax.ShapeDtypeStruct((1, h, width), jnp.bfloat16)] * 3
        out_specs = [pl.BlockSpec((1, h, tile), lambda n: (0, 0, n))] * 3
        in_specs = in_specs + [three]
    return pl.pallas_call(
        kernel,
        out_shape=outs,
        grid=(width // tile,),
        in_specs=in_specs,
        out_specs=out_specs,
        compiler_params=pltpu.CompilerParams(vmem_limit_bytes=VMEM_LIMIT),
        cost_estimate=cost(),
        name=name,
    )(*wide, *narrow, *more)


def all_slots_body(tokens, routes, route_weight, w_gate, w_up, w_down, grad_out):
    f32 = jnp.float32
    dp_count = lax.axis_size("dp")
    ex_count = lax.axis_size("expert")
    levels = ex_count // CORES
    groups = ex_count // SHARDS
    width = tokens.shape[1]
    block = grad_out.shape[0]
    half = levels * block
    dp_index = lax.axis_index("dp")
    ex_index = lax.axis_index("expert")
    level, core = ex_index // CORES, ex_index % CORES

    def pieces(values):
        rest, parts = values.reshape(-1), []
        for _ in range(3):
            part = lax.reduce_precision(rest, 8, 7)
            parts.append(part.astype(jnp.bfloat16))
            rest = rest - part
        row = jnp.concatenate(parts)
        row = jnp.pad(row, (0, PACKED_ROWS * width - row.shape[0]))
        return row.reshape(PACKED_ROWS, width)

    def whole(message, position):
        row = message[half : half + PACKED_ROWS].reshape(-1)[: 9 * half]
        parts = row.reshape(3, 3, half)[:, position].astype(f32)
        return (parts[0] + parts[1]) + parts[2]

    def exchange(value, partner):
        pairs = []
        for d in range(dp_count):
            for e in range(ex_count):
                other_d, other_e = partner(d, e // CORES, e % CORES)
                pairs.append((d * ex_count + e, other_d * ex_count + other_e))
        return lax.ppermute(value, ("dp", "expert"), pairs)

    def to_near(value):
        return exchange(value, lambda d, z, c: (d ^ (1 + c), z * CORES + c))

    def to_far(value):
        return exchange(value, lambda d, z, c: (d ^ (2 - c), z * CORES + c))

    def to_core(value):
        return exchange(value, lambda d, z, c: (d, z * CORES + 1 - c))

    def to_level(value, step):
        return exchange(value, lambda d, z, c: (d, (z ^ step) * CORES + c))

    def add(*terms):
        total = terms[0].astype(f32)
        for term in terms[1:]:
            total = total + term.astype(f32)
        return total.astype(terms[0].dtype)

    def after(value, *others):
        return lax.optimization_barrier((value, *others))[0]

    def in_blocks(terms):
        return [term.reshape(levels, block, term.shape[-1]) for term in terms]

    def by_blocks(terms, *wait_for):
        terms = in_blocks(terms)
        received = [
            to_level(add(*[term[k] for term in terms]), step)
            for k, step in enumerate(LEVEL_STEPS)
            if k > 0
        ]
        own = after(terms[0][0], *wait_for)
        return add(own, *[term[0] for term in terms[1:]], *received)

    level_order = jnp.array(LEVEL_STEPS, jnp.int32) ^ level
    block_order = level_order * CORES + core
    near, far = dp_index ^ (1 + core), dp_index ^ (2 - core)
    group_dp = (dp_index, near, far, dp_index ^ 3)

    group_experts = jnp.arange(dp_count, dtype=jnp.int32) * groups + ex_index // SHARDS
    table = jnp.sum(
        jnp.where(routes[None] == group_experts[:, None, None], route_weight[None], 0.0), axis=2
    )
    table = table.reshape(dp_count, ex_count, block)[:, block_order]
    own_table, near_table, far_table, diagonal_table = (
        lax.dynamic_index_in_dim(table, d, axis=0).reshape(half) for d in group_dp
    )

    x_own = tokens.reshape(ex_count, block, width)[block_order].reshape(half, width)
    x_own = jnp.concatenate(
        [x_own, pieces(jnp.stack([near_table, far_table, diagonal_table]))], axis=0
    )
    x_near = to_near(x_own)
    x_far = to_far(x_own)
    others = [to_core(matrix) for matrix in (w_gate, w_up, w_down)]
    matrices = (w_gate, others[0], w_up, others[1], w_down, others[2])
    cotangent = after(grad_out, x_own)
    g_pair = jnp.concatenate([cotangent, to_level(cotangent, 2)], axis=0)
    x_last = to_far(after(x_near, x_far))
    weight12 = jnp.concatenate([own_table, whole(x_near, 0)])[:, None]
    weight34 = jnp.concatenate([whole(x_far, 1), whole(x_last, 2)])[:, None]

    mixed12, hidden12, weighted12, *slopes12 = forward(matrices, (x_own, x_near), weight12)
    x_last = after(x_last, mixed12)
    g_own = jnp.concatenate([g_pair, to_level(g_pair, 1)], axis=0)
    g_own = after(g_own, x_near, x_far)
    g_near = to_near(g_own)
    g_far = to_far(after(g_own, x_last, g_near))
    g_last = to_far(after(g_near, x_last))
    ahead, back = middle(
        matrices, (x_far, x_last), (g_own, g_near), weight34, weight12, (hidden12, *slopes12)
    )
    mixed34, hidden34, weighted34, *slopes34 = ahead
    dx12, route12, gate12, up12 = back
    g_last = after(g_last, mixed34)
    dx34, route34, gate34, up34 = backward(
        matrices, (g_far, g_last), weight34, (hidden34, *slopes34)
    )

    mixed_far = to_far(after(mixed34, g_far, g_last))
    mixed_part = add(mixed12[half:], after(mixed_far, dx34)[half:])
    mixed_near = to_near(mixed_part)

    h = w_gate.shape[1]
    wide = (x_own, x_near, x_far, x_last, g_own, g_near, g_far, g_last)
    narrow = after((gate12, gate34, up12, up34, weighted12, weighted34), mixed_far)
    for_other = weight_grads(wide, narrow, h)
    grads = weight_grads(wide, narrow, h, to_core(for_other))
    mixed_near = after(mixed_near, for_other)


    mixed_terms = in_blocks((mixed12[:half], mixed_far[:half], mixed_near))
    mixed_pair = add(*[term[2:] for term in mixed_terms])
    mixed_pair = to_level(mixed_pair, 1)
    mixed_last = to_level(add(*[term[1] for term in mixed_terms], mixed_pair[1]), 2)
    dx_far = after(to_far(after(dx34, mixed_near)), mixed_pair)
    dx_part = add(dx12[half:], dx_far[half:])
    dx_near = to_near(dx_part)
    dx_near = after(dx_near, mixed_last)

    route = jnp.concatenate([route12, route34]).reshape(dp_count, levels, block)
    pair = after(to_level(route[:, 2:], 1), mixed_part)
    other_group = after(to_level(route[:, 1] + pair[:, 1], 2), dx_near)
    route = jnp.stack([route[:, 0] + pair[:, 0], other_group], axis=1)
    route_far = after(to_far(route[2:]), dx_near)
    route_near = to_near(jnp.stack([route[1], route_far[1]]))

    mixed_last = after(mixed_last, *grads)
    mixed = add(*[term[0] for term in mixed_terms], mixed_pair[0], mixed_last)
    grad_tokens = by_blocks((dx12[:half], dx_far[:half], dx_near), *grads)

    route_own = jnp.stack([route[0], route_far[0], route_near[0], route_near[1]])
    my_routes = lax.dynamic_slice_in_dim(routes, ex_index * block, block, axis=0)
    my_group = ex_index // SHARDS
    grad_route = jnp.zeros(my_routes.shape, f32)
    for which, group in enumerate((my_group, 1 - my_group)):
        for position, d in enumerate((dp_index, far, near, dp_index ^ 3)):
            grad_route = grad_route + jnp.where(
                my_routes == d * groups + group, route_own[position, which][:, None], 0.0
            )
    return (mixed, grad_tokens, grad_route, *grads)


def body(tokens, routes, *rest):
    dp_count = lax.axis_size("dp")
    ex_count = lax.axis_size("expert")
    tok_rows, top_count = routes.shape
    expert_count = dp_count * ex_count // SHARDS
    every_slot = 3 * tok_rows * top_count >= 2 * expert_count * tok_rows
    if every_slot and dp_count == 4 and ex_count == CORES * len(LEVEL_STEPS):
        return all_slots_body(tokens, routes, *rest)
    return padded_body(tokens, routes, *rest)


def solution(mesh):
    return jax.shard_map(
        body,
        mesh=mesh,
        in_specs=(
            P("dp", None),
            P("dp", None),
            P("dp", None),
            P(("dp", "expert"), None, None),
            P(("dp", "expert"), None, None),
            P(("dp", "expert"), None, None),
            P(("dp", "expert"), None),
        ),
        out_specs=(
            P(("dp", "expert"), None),
            P(("dp", "expert"), None),
            P(("dp", "expert"), None),
            P(("dp", "expert"), None, None),
            P(("dp", "expert"), None, None),
            P(("dp", "expert"), None, None),
        ),
        check_vma=False,
    )
```
